32 devices in a mesh: span: 4 (over y, x), leaf: 8 (over z, core).
Axes of the slice: x: 2, y: 2, z: 4, core: 2. Of those that a mesh axis runs over, the one named last changes fastest.
Arguments:
- populations: float32 [27, 64, 64, 128], P(None, 'span', 'leaf'), may hold values from 0.5 to 1.5
- relax_rates: float32 [27], replicated, may hold values from 1 to 1.6
- marker_forces: float32 [2, 3, 12288], P(None, None, ('span', 'leaf')), may hold values from -6 to 6
- marker_dest: int32 [2, 12288, 1], P(None, ('span', 'leaf')), may hold values from 0 to 7; in each aligned block of 384 rows (0 to 383, 384 to 767, ..., all dimensions but the last counted through in order) at most 144 rows name the same one
- marker_cells: int32 [2, 12288], P(None, ('span', 'leaf')), may hold values from 0 to 16383
Outputs:
- final_state: float32 [27, 64, 64, 128], P(None, 'span', 'leaf')
The draws below stay inside these ranges and needn't reach their ends.
Inputs may be any that keep to these rules, and one draw needn't show every extreme that they name: `marker_dest`: in each step, no destination is named by more than 144 of the 384 markers of one device, and in every draw some device's markers name one destination exactly 144 times.
All inputs are finite; a program needn't handle non-finite values.
Results may differ from the reference program's by a relative error of at most 0.0001.
Values sent between devices are 32-bit elements; how exact they have to be, the bound alone decides.
A program may use at most 64 MiB of HBM per device.

```python
import math
import jax
import jax.numpy as jnp
import numpy as np
from jax import lax

CX = 16
CZ = 8
NY = 128
MARK_DEV = 384
STEPS = 2
CAP = 144
CELLS = 16384
NX = 64
NZ = 64
GROUP_MARKERS = 3072
MARKERS = 12288
N_LEAF = 8


def set_ends(result, own_key, smallest, top_value):
    index_at = [jax.random.randint(jax.random.fold_in(own_key, axis), (), 0, length) for axis, length in enumerate(result.shape)]
    longest = result.shape.index(max(result.shape))
    next_to = index_at[:longest] + [(index_at[longest] + 1) % result.shape[longest]] + index_at[longest + 1:]
    return result.at[tuple(index_at)].set(smallest).at[tuple(next_to)].set(top_value)


def levels(own_key, dims, split, least, top_value):
    loudness, own = 1.0, jax.random.fold_in(own_key, 6)
    for axis_at, shards_of in split:
        heights = jnp.exp(jax.random.uniform(jax.random.fold_in(own, axis_at), (shards_of,), jnp.float32, least / len(split), top_value / len(split)))
        loudness = loudness * jnp.repeat(heights, dims[axis_at] // shards_of).reshape([-1 if axis == axis_at else 1 for axis in range(len(dims))])
    return loudness


def deal_out(key, own, number, rows, number_of, top, reach, lean):
    order = jax.random.permutation(key, number_of)
    packed, common = portions_of(number_of, rows * top, reach, lean, True), portions_of(number_of, rows * top, reach, lean, False)
    places = jnp.arange(number_of)

    def named(lengths, turn):
        used = int((lengths > 0).sum())
        fixed = max(1, used // 4)
        shifted = fixed + (places - fixed + turn * (used - fixed)) % max(1, number_of - fixed)
        return jnp.zeros((number_of,), jnp.int32).at[order[jnp.where(places < fixed, places, shifted)]].set(jnp.asarray(lengths, jnp.int32))

    lengths = jnp.where(number % 4 == 0, named(packed, number // 4), named(common, number - number // 4 - 1))
    mixed = jax.random.permutation(jax.random.fold_in(own, 3), number_of)
    giver, receiver = mixed[0:number_of // 2 * 2:2], mixed[1:number_of // 2 * 2:2]
    margin = jnp.minimum(lengths[giver] - 1, reach - lengths[receiver]) // 2
    margin = jnp.where((giver == order[0]) | (receiver == order[0]) | (lengths[receiver] == 0), 0, jnp.maximum(margin, 0))
    shifted = jax.random.randint(jax.random.fold_in(own, 4), (number_of // 2,), 0, 1 << 20) % (margin + 1)
    lengths = lengths.at[giver].add(-shifted).at[receiver].add(shifted)
    items = jnp.searchsorted(jnp.cumsum(lengths), jnp.arange(rows * top), side="right").astype(jnp.int32)
    listing = items.reshape(top, rows).T
    listing = listing[jax.random.permutation(jax.random.fold_in(own, 1), rows)]
    turn = jax.random.randint(jax.random.fold_in(own, 2), (rows, 1), 0, top)
    return jnp.take_along_axis(listing, (jnp.arange(top)[None, :] + turn) % top, axis=1)


def portions_of(amount, total, reach, skew, full):
    portions = [(1 << 20) // math.isqrt(standing ** skew) + 1 for standing in range(1, amount + 1)]
    largest = reach if full else min(reach, max(-(-total // amount), total * portions[0] // sum(portions)))
    least = 1 if total - largest >= amount - 1 else 0
    given, spare = [largest] + [least] * (amount - 1), total - largest - least * (amount - 1)
    while spare > 0:
        movable = [i for i in range(1, amount) if given[i] < largest] or [i for i in range(1, amount) if given[i] < reach]
        whole, remaining = sum([portions[i] for i in movable]), spare
        for i in movable:
            addition = min(reach - given[i], max(1, remaining * portions[i] // whole), spare)
            given[i] = given[i] + addition
            spare = spare - addition
    return np.array(given)


def centred(rng, dims, spread, limit, split=(), kind=jnp.bfloat16):
    loudness = levels(rng, dims, split, -0.22, 0.18) if split else 1.0
    drawn = jax.random.normal(rng, dims, jnp.float32) * spread * loudness
    return jnp.minimum(jnp.maximum(drawn, -limit), limit).astype(kind)


def setup_inputs(seed: int = 0) -> dict:
    streams_of = jax.random.split(jax.random.key(seed), 6)
    populations = jnp.clip(0.5 + 1.0 * jax.random.uniform(streams_of[0], (27, NX, NZ, NY), jnp.float32) ** levels(streams_of[0], (27, NX, NZ, NY), ((1, 4), (2, 8)), -0.2, 0.2), 0.5, 1.5)
    relax_rates = jnp.clip(jnp.exp(jax.random.uniform(streams_of[1], (27,), jnp.float32, math.log(1.0), math.log(1.6))), 1.0, 1.6)
    marker_forces = centred(streams_of[2], (STEPS, 3, MARKERS), 1.0, 6.0, ((2, 32),), jnp.float32)
    marker_dest_keys = jax.random.split(jax.random.fold_in(streams_of[3], 1), STEPS * MARKERS // MARK_DEV)
    marker_dest_turns = jax.random.permutation(jax.random.fold_in(streams_of[3], 3), STEPS * MARKERS // MARK_DEV)
    marker_dest = jax.vmap(lambda own, number: deal_out(jax.random.fold_in(streams_of[3], 2), own, number, MARK_DEV, N_LEAF, 1, CAP, 2))(marker_dest_keys, marker_dest_turns).reshape((STEPS, MARKERS, 1))
    marker_cells = set_ends(jax.random.randint(streams_of[4], (STEPS, MARKERS), 0, CELLS), jax.random.fold_in(streams_of[4], 1), 0, CELLS - 1).astype(jnp.int32)
    return dict(populations=populations, relax_rates=relax_rates, marker_forces=marker_forces, marker_dest=marker_dest, marker_cells=marker_cells)


RHO_BASE = 27.0


def lattice_tables():
    axis_values = np.array([-1.0, 0.0, 1.0])
    powers = np.array([[1.0, 1.0, 1.0], [-1.0, 0.0, 1.0], [1.0, 0.0, 1.0]])
    inverse = np.array([[0.0, -0.5, 0.5], [1.0, 0.0, -1.0], [0.0, 0.5, 0.5]])
    forward = np.kron(np.kron(powers, powers), powers)
    backward = np.kron(np.kron(inverse, inverse), inverse)
    one_weight = np.array([1.0 / 6.0, 2.0 / 3.0, 1.0 / 6.0])
    weights = np.kron(np.kron(one_weight, one_weight), one_weight)
    velocity = np.stack(np.meshgrid(axis_values, axis_values, axis_values, indexing="ij"), 0).reshape(3, 27)
    return forward, backward, weights, velocity


def collide(populations, rates_cell, force_field, tables):
    forward = jnp.asarray(tables[0], dtype=jnp.float32)
    backward = jnp.asarray(tables[1], dtype=jnp.float32)
    weights = jnp.asarray(tables[2], dtype=jnp.float32)
    velocity = jnp.asarray(tables[3], dtype=jnp.float32)
    highest = lax.Precision.HIGHEST
    density = jnp.sum(populations, axis=0)
    momentum = jnp.einsum("dq,q...->d...", velocity, populations, precision=highest)
    velocity_field = momentum / RHO_BASE
    along = jnp.einsum("dq,d...->q...", velocity, velocity_field, precision=highest)
    square = jnp.sum(velocity_field * velocity_field, axis=0)
    shaped = weights.reshape((27,) + (1,) * (populations.ndim - 1))
    equilibrium = shaped * (density + RHO_BASE * (3.0 * along + 4.5 * along * along - 1.5 * square))
    moments = jnp.einsum("kq,q...->k...", forward, populations - equilibrium, precision=highest)
    relaxed = jnp.einsum("qk,k...->q...", backward, rates_cell * moments, precision=highest)
    source = 3.0 * shaped * jnp.einsum("dq,d...->q...", velocity, force_field, precision=highest)
    return populations - relaxed + source


def stream_whole(post, velocity):
    moved = []
    for direction in range(27):
        shift_x = int(velocity[0, direction])
        shift_y = int(velocity[1, direction])
        shift_z = int(velocity[2, direction])
        moved.append(jnp.roll(post[direction], (shift_x, shift_z, shift_y), axis=(0, 1, 2)))
    return jnp.stack(moved)


def reference(populations, relax_rates, marker_forces, marker_dest, marker_cells):
    tables = lattice_tables()
    rates_cell = relax_rates[:, None, None, None]
    marker_ids = jnp.arange(MARKERS, dtype=jnp.int32)
    span_ids = marker_ids // GROUP_MARKERS
    state = populations
    for time_step in range(STEPS):
        cell_ids = marker_cells[time_step]
        row_x = span_ids * CX + cell_ids // (CZ * NY)
        row_z = marker_dest[time_step, :, 0] * CZ + (cell_ids // NY) % CZ
        row_y = cell_ids % NY
        force_field = jnp.zeros((3, NX, NZ, NY), jnp.float32).at[:, row_x, row_z, row_y].add(marker_forces[time_step])
        post = collide(state, rates_cell, force_field, tables)
        state = stream_whole(post, tables[3])
    return state
```

```python
import functools

import jax
import jax.numpy as jnp
from jax import lax
from jax.experimental import pallas as pl
from jax.experimental.pallas import tpu as pltpu
from jax.sharding import PartitionSpec as P

MESH = pl.DeviceIdType.MESH
F32 = jnp.float32
BF16 = jnp.bfloat16


def parts(index):
    return index // 9, (index // 3) % 3, index % 3


def forward(values):
    for stride in (1, 3, 9):
        moved = list(values)
        for low in range(27):
            if (low // stride) % 3 == 0:
                a, b, c = (values[low + stride * i] for i in range(3))
                both = a + c
                moved[low] = both + b
                moved[low + stride] = c - a
                moved[low + 2 * stride] = both
        values = moved
    return values


def backward(values):
    for stride in (9, 3, 1):
        moved = list(values)
        for low in range(27):
            if (low // stride) % 3 == 0:
                a, b, c = (values[low + stride * i] for i in range(3))
                moved[low] = c - b
                moved[low + stride] = a - (c + c)
                moved[low + 2 * stride] = c + b
        values = moved
    return values


def relax(m, keep, pull):
    momentum = (m[9], m[3], m[1])
    squares = [v * v * (1.0 / 9.0) for v in momentum]
    result = []
    for k in range(27):
        power = parts(k)
        ones = [i for i in range(3) if power[i] == 1]
        if len(ones) == 3:
            result.append(keep(k) * m[k])
            continue
        if len(ones) == 2:
            target = momentum[ones[0]] * momentum[ones[1]] * (1.0 / 27.0)
        elif len(ones) == 1:
            target = momentum[ones[0]]
        else:
            target = m[0]
            for i in range(3):
                if power[i] == 2:
                    target = target + squares[i]
        result.append(keep(k) * m[k] + pull(k) * target)
    return result


def add_force(n, force):
    n = list(n)
    for k in range(27):
        power = parts(k)
        ones = [i for i in range(3) if power[i] == 1]
        if len(ones) == 1:
            twos = sum(1 for p in power if p == 2)
            factor = 0.5 * (0.5 / 3.0) ** twos
            n[k] = n[k] + factor * force[ones[0]]
    return n


def kernel(
    spans, leaves,
    pop, rates, forces, dest, cells, out,
    f, pa, pb, coef, force, hot_a, hot_b,
    m_forces, m_dest, m_cells, m_send, m_recv,
    send_p, send_m, zlo, zhi,
    in_sem, out_sem, ms_sem, mr_sem, hs_sem, hr_sem,
):
    wx = pop.shape[1]
    count = cells.shape[1]
    me_s = lax.axis_index("span")
    me_l = lax.axis_index("leaf")

    def device(ds, dl):
        return (lax.rem(me_s + ds + spans, spans), lax.rem(me_l + dl + leaves, leaves))

    small = [
        pltpu.make_async_copy(forces, m_forces, in_sem.at[1]),
        pltpu.make_async_copy(dest, m_dest, in_sem.at[2]),
        pltpu.make_async_copy(cells, m_cells, in_sem.at[3]),
    ]
    for copy in small:
        copy.start()
    load = pltpu.make_async_copy(pop, f, in_sem.at[0])
    load.start()

    barrier = pltpu.get_barrier_semaphore()
    greeted = [(0, k) for k in range(1, leaves)]
    greeted += [(ds, dl) for ds in (1, -1) for dl in (0, 1, -1)]
    for ds, dl in greeted:
        pl.semaphore_signal(barrier, inc=1, device_id=device(ds, dl), device_id_type=MESH)

    for k in range(27):
        power = parts(k)
        scale = 0.5 ** sum(1 for p in power if p)
        third = (1.0 / 3.0) ** sum(1 for p in power if p == 2)
        rate = rates[k]
        coef[0, k] = jnp.full((8, 128), (1.0 - rate) * scale, F32)
        coef[1, k] = jnp.full((8, 128), rate * (scale * third), F32)

    for copy in small:
        copy.wait()
    for t in range(2):
        own_dest = m_dest[t]
        own_cells = m_cells[t : t + 1, :].astype(F32)
        own_force = m_forces[:, t, :]
        for k in range(leaves):
            chosen = own_dest == device(0, k)[1]
            masked = jnp.where(chosen, own_force, 0.0)
            target = m_recv if k == 0 else m_send
            target[t, k, 0:3, :] = masked
            target[t, k, 3:4, :] = own_cells
    pl.semaphore_wait(barrier, len(greeted))

    def marker_copy(t, k):
        return pltpu.make_async_remote_copy(
            src_ref=m_send.at[t, k], dst_ref=m_recv.at[t, k],
            send_sem=ms_sem.at[t, k], recv_sem=mr_sem.at[t, k],
            device_id=device(0, k), device_id_type=MESH,
        )

    for t in range(2):
        for k in range(1, leaves):
            marker_copy(t, k).start()

    def keep(k):
        return coef[0, k]

    def pull(k):
        return coef[1, k]

    load.wait()

    def relax_plane(x, carry):
        n = relax(forward([f[q, x] for q in range(27)]), keep, pull)
        for k in range(27):
            f[k, x] = n[k]
        return carry

    lax.fori_loop(0, wx, relax_plane, 0)

    def deposit(t):
        def spread(s):
            cell = m_recv[t, s, 3:4, :].astype(jnp.int32)
            row = (cell >> 7) & 63
            column = ((cell >> 13) << 7) + (cell & 127)
            lanes = pl.ds(pl.multiple_of(s * count, 128), count)
            is_column = lax.broadcasted_iota(jnp.int32, (256, count), 0) == column
            hot_b[:, lanes] = jnp.where(is_column, 1.0, 0.0).astype(BF16)
            is_row = lax.broadcasted_iota(jnp.int32, (64, count), 0) == row
            for d in range(3):
                amount = m_recv[t, s, d : d + 1, :]
                high = amount.astype(BF16).astype(F32)
                low = amount - high
                hot_a[64 * d : 64 * d + 64, lanes] = jnp.where(is_row, high, 0.0).astype(BF16)
                hot_a[192 + 64 * d : 256 + 64 * d, lanes] = jnp.where(is_row, low, 0.0).astype(BF16)

        spread(0)

        def arrived(s, carry):
            marker_copy(t, s).wait_recv()
            spread(s)
            return carry

        lax.fori_loop(1, leaves, arrived, 0)
        both = lax.dot_general(
            hot_a[...], hot_b[...], (((1,), (1,)), ((), ())), preferred_element_type=F32
        )
        total = both[0:192] + both[192:384]
        for d in range(3):
            for side in range(2):
                block = total[64 * d : 64 * d + 64, 128 * side : 128 * side + 128]
                force[d, 8 * side : 8 * side + 8] = block.reshape(8, 8, 128)

    def put(t, post, x, n):
        n = add_force(n, [force[d, x] for d in range(3)])
        values = backward(n)
        for q in range(27):
            _, cy, cz = parts(q)
            v = values[q]
            if cy != 1:
                v = pltpu.roll(v, 1 if cy == 2 else 127, axis=1)
            if cz != 1:
                v = pltpu.roll(v, 1 if cz == 2 else 7, axis=0)
            post[q, x + 1] = v
            if cz == 2:
                send_p[t, q // 3, x] = v[0:1]
            if cz == 0:
                send_m[t, q // 3, x] = v[7:8]

    def halo(t, post):
        low, high = zlo.at[t], zhi.at[t]
        up, down = send_p.at[t], send_m.at[t]
        last = wx - 1
        plan = [
            (post.at[18:27, wx], post.at[18:27, 0], (1, 0)),
            (post.at[0:9, 1], post.at[0:9, wx + 1], (-1, 0)),
            (up, low.at[:, 1 : wx + 1], (0, 1)),
            (down, high.at[:, 1 : wx + 1], (0, -1)),
            (up.at[6:9, last], low.at[6:9, 0], (1, 1)),
            (up.at[0:3, 0], low.at[0:3, wx + 1], (-1, 1)),
            (down.at[6:9, last], high.at[6:9, 0], (1, -1)),
            (down.at[0:3, 0], high.at[0:3, wx + 1], (-1, -1)),
        ]
        return [
            pltpu.make_async_remote_copy(
                src_ref=source, dst_ref=target,
                send_sem=hs_sem.at[t, i], recv_sem=hr_sem.at[t, i],
                device_id=device(*where), device_id_type=MESH,
            )
            for i, (source, target, where) in enumerate(plan)
        ]

    sublane = lax.broadcasted_iota(jnp.int32, (8, 128), 0)

    deposit(0)

    def put_plane(x, carry):
        put(0, pa, x, [f[k, x] for k in range(27)])
        return carry

    lax.fori_loop(0, wx, put_plane, 0)
    first = halo(0, pa)
    for copy in first:
        copy.start()
    deposit(1)
    for copy in first:
        copy.wait_recv()

    def whole_plane(x, carry):
        values = []
        for q in range(27):
            cx, _, cz = parts(q)
            at = x + (2 - cx)
            v = pa[q, at]
            if cz == 2:
                v = jnp.where(sublane == 0, zlo[0, q // 3, at], v)
            if cz == 0:
                v = jnp.where(sublane == 7, zhi[0, q // 3, at], v)
            values.append(v)
        put(1, pb, x, relax(forward(values), keep, pull))
        return carry

    lax.fori_loop(0, wx, whole_plane, 0)
    second = halo(1, pb)
    for copy in second:
        copy.start()
    for copy in second:
        copy.wait_recv()
    for copy in second:
        copy.wait_send()

    def close_plane(x, carry):
        for q in range(27):
            cx, _, cz = parts(q)
            at = x + (2 - cx)
            if cz == 2:
                pb[q, at, 0:1] = zlo[1, q // 3, at]
            if cz == 0:
                pb[q, at, 7:8] = zhi[1, q // 3, at]
        return carry

    lax.fori_loop(0, wx, close_plane, 0)
    stores = [
        pltpu.make_async_copy(
            pb.at[9 * c : 9 * c + 9, 2 - c : 2 - c + wx], out.at[9 * c : 9 * c + 9], out_sem.at[c]
        )
        for c in range(3)
    ]
    for copy in stores:
        copy.start()
    for copy in first:
        copy.wait_send()
    for t in range(2):
        for k in range(1, leaves):
            marker_copy(t, k).wait_send()
    for copy in stores:
        copy.wait()


def body(spans, leaves, populations, relax_rates, marker_forces, marker_dest, marker_cells):
    steps, _, count = marker_forces.shape
    wx = populations.shape[1]
    anywhere = pl.BlockSpec(memory_space=pl.ANY)
    vmem = pltpu.VMEM
    dma = pltpu.SemaphoreType.DMA
    return pl.pallas_call(
        functools.partial(kernel, spans, leaves),
        out_shape=jax.ShapeDtypeStruct(populations.shape, F32),
        in_specs=[anywhere, pl.BlockSpec(memory_space=pltpu.SMEM), anywhere, anywhere, anywhere],
        out_specs=anywhere,
        scratch_shapes=[
            vmem(populations.shape, F32),
            vmem((27, wx + 2, 8, 128), F32),
            vmem((27, wx + 2, 8, 128), F32),
            vmem((2, 27, 8, 128), F32),
            vmem((3, wx, 8, 128), F32),
            vmem((384, leaves * count), BF16),
            vmem((256, leaves * count), BF16),
            vmem((3, steps, count), F32),
            vmem((steps, 1, count), jnp.int32),
            vmem((steps, count), jnp.int32),
            vmem((steps, leaves, 4, count), F32),
            vmem((steps, leaves, 4, count), F32),
            vmem((steps, 9, wx, 1, 128), F32),
            vmem((steps, 9, wx, 1, 128), F32),
            vmem((steps, 9, wx + 2, 1, 128), F32),
            vmem((steps, 9, wx + 2, 1, 128), F32),
            dma((4,)),
            dma((3,)),
            dma((steps, leaves)),
            dma((steps, leaves)),
            dma((steps, 8)),
            dma((steps, 8)),
        ],
        compiler_params=pltpu.CompilerParams(
            collective_id=0, has_side_effects=True, vmem_limit_bytes=56 * 1024 * 1024
        ),
        cost_estimate=pl.CostEstimate(
            flops=700 * 2 * populations.size // 27, bytes_accessed=8 * populations.size,
            transcendentals=0,
        ),
    )(
        populations, relax_rates, marker_forces.transpose(1, 0, 2),
        marker_dest.transpose(0, 2, 1), marker_cells,
    )


def solution(mesh):
    spans, leaves = mesh.shape["span"], mesh.shape["leaf"]
    placed = (
        P(None, "span", "leaf", None),
        P(),
        P(None, None, ("span", "leaf")),
        P(None, ("span", "leaf"), None),
        P(None, ("span", "leaf")),
    )
    return jax.shard_map(
        functools.partial(body, spans, leaves),
        mesh=mesh, in_specs=placed, out_specs=P(None, "span", "leaf", None), check_vma=False,
    )
```

```python
import functools

import jax
import jax.numpy as jnp
from jax import lax
from jax.experimental import pallas as pl
from jax.experimental.pallas import tpu as pltpu
from jax.sharding import PartitionSpec as P

MESH = pl.DeviceIdType.MESH
F32 = jnp.float32
BF16 = jnp.bfloat16


def parts(index):
    return index // 9, (index // 3) % 3, index % 3


def forward(values):
    for stride in (1, 3, 9):
        moved = list(values)
        for low in range(27):
            if (low // stride) % 3 == 0:
                a, b, c = (values[low + stride * i] for i in range(3))
                both = a + c
                moved[low] = both + b
                moved[low + stride] = c - a
                moved[low + 2 * stride] = both
        values = moved
    return values


def backward(values):
    for stride in (9, 3, 1):
        moved = list(values)
        for low in range(27):
            if (low // stride) % 3 == 0:
                a, b, c = (values[low + stride * i] for i in range(3))
                moved[low] = c - b
                moved[low + stride] = a - (c + c)
                moved[low + 2 * stride] = c + b
        values = moved
    return values


def relax(m, keep, pull):
    momentum = (m[9], m[3], m[1])
    squares = [v * v * (1.0 / 9.0) for v in momentum]
    result = []
    for k in range(27):
        power = parts(k)
        ones = [i for i in range(3) if power[i] == 1]
        if len(ones) == 3:
            result.append(keep(k) * m[k])
            continue
        if len(ones) == 2:
            target = momentum[ones[0]] * momentum[ones[1]] * (1.0 / 27.0)
        elif len(ones) == 1:
            target = momentum[ones[0]]
        else:
            target = m[0]
            for i in range(3):
                if power[i] == 2:
                    target = target + squares[i]
        result.append(keep(k) * m[k] + pull(k) * target)
    return result


def add_force(n, force):
    n = list(n)
    for k in range(27):
        power = parts(k)
        ones = [i for i in range(3) if power[i] == 1]
        if len(ones) == 1:
            twos = sum(1 for p in power if p == 2)
            factor = 0.5 * (0.5 / 3.0) ** twos
            n[k] = n[k] + factor * force[ones[0]]
    return n


def kernel(
    spans, leaves,
    pop, rates, forces, dest, cells, out,
    f, pa, pb, coef, force, hot_a, hot_b,
    m_forces, m_dest, m_cells, m_send, m_recv,
    send_p, send_m, zlo, zhi,
    in_sem, ms_sem, mr_sem, hs_sem, hr_sem,
):
    wx = pop.shape[1]
    count = cells.shape[1]
    me_s = lax.axis_index("span")
    me_l = lax.axis_index("leaf")

    def device(ds, dl):
        return (lax.rem(me_s + ds + spans, spans), lax.rem(me_l + dl + leaves, leaves))

    small = [
        pltpu.make_async_copy(forces, m_forces, in_sem.at[1]),
        pltpu.make_async_copy(dest, m_dest, in_sem.at[2]),
        pltpu.make_async_copy(cells, m_cells, in_sem.at[3]),
    ]
    for copy in small:
        copy.start()
    load = pltpu.make_async_copy(pop, f, in_sem.at[0])
    load.start()

    barrier = pltpu.get_barrier_semaphore()
    greeted = [(0, k) for k in range(1, leaves)]
    greeted += [(ds, dl) for ds in (1, -1) for dl in (0, 1, -1)]
    for ds, dl in greeted:
        pl.semaphore_signal(barrier, inc=1, device_id=device(ds, dl), device_id_type=MESH)

    for k in range(27):
        power = parts(k)
        scale = 0.5 ** sum(1 for p in power if p)
        third = (1.0 / 3.0) ** sum(1 for p in power if p == 2)
        rate = rates[k]
        coef[0, k] = jnp.full((8, 128), (1.0 - rate) * scale, F32)
        coef[1, k] = jnp.full((8, 128), rate * (scale * third), F32)

    for copy in small:
        copy.wait()
    for t in range(2):
        own_dest = m_dest[t]
        own_cells = m_cells[t : t + 1, :].astype(F32)
        own_force = m_forces[:, t, :]
        for k in range(leaves):
            chosen = own_dest == device(0, k)[1]
            masked = jnp.where(chosen, own_force, 0.0)
            target = m_recv if k == 0 else m_send
            target[t, k, 0:3, :] = masked
            target[t, k, 3:4, :] = own_cells
    pl.semaphore_wait(barrier, len(greeted))

    def marker_copy(t, k):
        return pltpu.make_async_remote_copy(
            src_ref=m_send.at[t, k], dst_ref=m_recv.at[t, k],
            send_sem=ms_sem.at[t, k], recv_sem=mr_sem.at[t, k],
            device_id=device(0, k), device_id_type=MESH,
        )

    for t in range(2):
        for k in range(1, leaves):
            marker_copy(t, k).start()

    def keep(k):
        return coef[0, k]

    def pull(k):
        return coef[1, k]

    load.wait()

    def relax_plane(x, carry):
        n = relax(forward([f[q, x] for q in range(27)]), keep, pull)
        for k in range(27):
            f[k, x] = n[k]
        return carry

    lax.fori_loop(0, wx, relax_plane, 0)

    def deposit(t):
        def spread(s):
            cell = m_recv[t, s, 3:4, :].astype(jnp.int32)
            row = (cell >> 7) & 63
            column = ((cell >> 13) << 7) + (cell & 127)
            lanes = pl.ds(pl.multiple_of(s * count, 128), count)
            is_column = lax.broadcasted_iota(jnp.int32, (256, count), 0) == column
            hot_b[:, lanes] = jnp.where(is_column, 1.0, 0.0).astype(BF16)
            is_row = lax.broadcasted_iota(jnp.int32, (64, count), 0) == row
            for d in range(3):
                amount = m_recv[t, s, d : d + 1, :]
                high = amount.astype(BF16).astype(F32)
                low = amount - high
                hot_a[64 * d : 64 * d + 64, lanes] = jnp.where(is_row, high, 0.0).astype(BF16)
                hot_a[192 + 64 * d : 256 + 64 * d, lanes] = jnp.where(is_row, low, 0.0).astype(BF16)

        spread(0)

        def arrived(s, carry):
            marker_copy(t, s).wait_recv()
            spread(s)
            return carry

        lax.fori_loop(1, leaves, arrived, 0)
        both = lax.dot_general(
            hot_a[...], hot_b[...], (((1,), (1,)), ((), ())), preferred_element_type=F32
        )
        total = both[0:192] + both[192:384]
        for d in range(3):
            for side in range(2):
                block = total[64 * d : 64 * d + 64, 128 * side : 128 * side + 128]
                force[d, 8 * side : 8 * side + 8] = block.reshape(8, 8, 128)

    def put(t, post, x, n):
        n = add_force(n, [force[d, x] for d in range(3)])
        values = backward(n)
        for q in range(27):
            _, cy, cz = parts(q)
            v = values[q]
            if cy != 1:
                v = pltpu.roll(v, 1 if cy == 2 else 127, axis=1)
            if cz != 1:
                v = pltpu.roll(v, 1 if cz == 2 else 7, axis=0)
            post[q, x + 1] = v
            if cz == 2:
                send_p[t, q // 3, x] = v[0:1]
            if cz == 0:
                send_m[t, q // 3, x] = v[7:8]

    def halo(t, post):
        low, high = zlo.at[t], zhi.at[t]
        up, down = send_p.at[t], send_m.at[t]
        last = wx - 1
        plan = [
            (post.at[18:27, wx], post.at[18:27, 0], (1, 0)),
            (post.at[0:9, 1], post.at[0:9, wx + 1], (-1, 0)),
            (up, low.at[:, 1 : wx + 1], (0, 1)),
            (down, high.at[:, 1 : wx + 1], (0, -1)),
            (up.at[6:9, last], low.at[6:9, 0], (1, 1)),
            (up.at[0:3, 0], low.at[0:3, wx + 1], (-1, 1)),
            (down.at[6:9, last], high.at[6:9, 0], (1, -1)),
            (down.at[0:3, 0], high.at[0:3, wx + 1], (-1, -1)),
        ]
        return [
            pltpu.make_async_remote_copy(
                src_ref=source, dst_ref=target,
                send_sem=hs_sem.at[t, i], recv_sem=hr_sem.at[t, i],
                device_id=device(*where), device_id_type=MESH,
            )
            for i, (source, target, where) in enumerate(plan)
        ]

    sublane = lax.broadcasted_iota(jnp.int32, (8, 128), 0)

    deposit(0)

    def put_plane(x, carry):
        put(0, pa, x, [f[k, x] for k in range(27)])
        return carry

    lax.fori_loop(0, wx, put_plane, 0)
    first = halo(0, pa)
    for copy in first:
        copy.start()
    deposit(1)
    for copy in first:
        copy.wait_recv()

    def whole_plane(x, carry):
        values = []
        for q in range(27):
            cx, _, cz = parts(q)
            at = x + (2 - cx)
            v = pa[q, at]
            if cz == 2:
                v = jnp.where(sublane == 0, zlo[0, q // 3, at], v)
            if cz == 0:
                v = jnp.where(sublane == 7, zhi[0, q // 3, at], v)
            values.append(v)
        put(1, pb, x, relax(forward(values), keep, pull))
        return carry

    lax.fori_loop(0, wx, whole_plane, 0)
    second = halo(1, pb)
    for copy in second:
        copy.start()
    for copy in second:
        copy.wait_recv()
    for copy in second:
        copy.wait_send()

    def close_plane(x, carry):
        for q in range(27):
            cx, _, cz = parts(q)
            at = x + (2 - cx)
            v = pb[q, at]
            if cz == 2:
                v = jnp.where(sublane == 0, zlo[1, q // 3, at], v)
            if cz == 0:
                v = jnp.where(sublane == 7, zhi[1, q // 3, at], v)
            out[q, x] = v
        return carry

    lax.fori_loop(0, wx, close_plane, 0)
    for copy in first:
        copy.wait_send()
    for t in range(2):
        for k in range(1, leaves):
            marker_copy(t, k).wait_send()


def body(spans, leaves, populations, relax_rates, marker_forces, marker_dest, marker_cells):
    steps, _, count = marker_forces.shape
    wx = populations.shape[1]
    anywhere = pl.BlockSpec(memory_space=pl.ANY)
    vmem = pltpu.VMEM
    dma = pltpu.SemaphoreType.DMA
    return pl.pallas_call(
        functools.partial(kernel, spans, leaves),
        out_shape=vmem(populations.shape, F32),
        in_specs=[anywhere, pl.BlockSpec(memory_space=pltpu.SMEM), anywhere, anywhere, anywhere],
        out_specs=pl.BlockSpec(memory_space=vmem),
        scratch_shapes=[
            vmem(populations.shape, F32),
            vmem((27, wx + 2, 8, 128), F32),
            vmem((27, wx + 2, 8, 128), F32),
            vmem((2, 27, 8, 128), F32),
            vmem((3, wx, 8, 128), F32),
            vmem((384, leaves * count), BF16),
            vmem((256, leaves * count), BF16),
            vmem((3, steps, count), F32),
            vmem((steps, 1, count), jnp.int32),
            vmem((steps, count), jnp.int32),
            vmem((steps, leaves, 4, count), F32),
            vmem((steps, leaves, 4, count), F32),
            vmem((steps, 9, wx, 1, 128), F32),
            vmem((steps, 9, wx, 1, 128), F32),
            vmem((steps, 9, wx + 2, 1, 128), F32),
            vmem((steps, 9, wx + 2, 1, 128), F32),
            dma((4,)),
            dma((steps, leaves)),
            dma((steps, leaves)),
            dma((steps, 8)),
            dma((steps, 8)),
        ],
        compiler_params=pltpu.CompilerParams(
            collective_id=0, has_side_effects=True, vmem_limit_bytes=60 * 1024 * 1024
        ),
        cost_estimate=pl.CostEstimate(
            flops=700 * 2 * populations.size // 27, bytes_accessed=8 * populations.size,
            transcendentals=0,
        ),
    )(
        populations, relax_rates, marker_forces.transpose(1, 0, 2),
        marker_dest.transpose(0, 2, 1), marker_cells,
    )


def solution(mesh):
    spans, leaves = mesh.shape["span"], mesh.shape["leaf"]
    placed = (
        P(None, "span", "leaf", None),
        P(),
        P(None, None, ("span", "leaf")),
        P(None, ("span", "leaf"), None),
        P(None, ("span", "leaf")),
    )
    return jax.shard_map(
        functools.partial(body, spans, leaves),
        mesh=mesh, in_specs=placed, out_specs=P(None, "span", "leaf", None), check_vma=False,
    )
```

```python
import functools

import jax
import jax.numpy as jnp
from jax import lax
from jax.experimental import pallas as pl
from jax.experimental.pallas import tpu as pltpu
from jax.sharding import PartitionSpec as P

MESH = pl.DeviceIdType.MESH
F32 = jnp.float32
BF16 = jnp.bfloat16


def parts(index):
    return index // 9, (index // 3) % 3, index % 3


def forward(values):
    for stride in (1, 3, 9):
        moved = list(values)
        for low in range(27):
            if (low // stride) % 3 == 0:
                a, b, c = (values[low + stride * i] for i in range(3))
                both = a + c
                moved[low] = both + b
                moved[low + stride] = c - a
                moved[low + 2 * stride] = both
        values = moved
    return values


def backward(values):
    for stride in (9, 3, 1):
        moved = list(values)
        for low in range(27):
            if (low // stride) % 3 == 0:
                a, b, c = (values[low + stride * i] for i in range(3))
                moved[low] = c - b
                moved[low + stride] = a - (c + c)
                moved[low + 2 * stride] = c + b
        values = moved
    return values


def relax(m, keep, pull):
    momentum = (m[9], m[3], m[1])
    squares = [v * v * (1.0 / 9.0) for v in momentum]
    result = []
    for k in range(27):
        power = parts(k)
        ones = [i for i in range(3) if power[i] == 1]
        if len(ones) == 3:
            result.append(keep(k) * m[k])
            continue
        if len(ones) == 2:
            target = momentum[ones[0]] * momentum[ones[1]] * (1.0 / 27.0)
        elif len(ones) == 1:
            target = momentum[ones[0]]
        else:
            target = m[0]
            for i in range(3):
                if power[i] == 2:
                    target = target + squares[i]
        result.append(keep(k) * m[k] + pull(k) * target)
    return result


def add_force(n, force):
    n = list(n)
    for k in range(27):
        power = parts(k)
        ones = [i for i in range(3) if power[i] == 1]
        if len(ones) == 1:
            twos = sum(1 for p in power if p == 2)
            factor = 0.5 * (0.5 / 3.0) ** twos
            n[k] = n[k] + factor * force[ones[0]]
    return n


def kernel(
    spans, leaves,
    pop, rates, forces, dest, cells, out,
    f, pa, pb, coef, force, hot_a, hot_b,
    m_forces, m_dest, m_cells, m_send, m_recv,
    send_p, send_m, zlo, zhi,
    in_sem, ms_sem, mr_sem, hs_sem, hr_sem,
):
    wx = pop.shape[1]
    count = cells.shape[1]
    me_s = lax.axis_index("span")
    me_l = lax.axis_index("leaf")

    def device(ds, dl):
        return (lax.rem(me_s + ds + spans, spans), lax.rem(me_l + dl + leaves, leaves))

    small = [
        pltpu.make_async_copy(forces, m_forces, in_sem.at[1]),
        pltpu.make_async_copy(dest, m_dest, in_sem.at[2]),
        pltpu.make_async_copy(cells, m_cells, in_sem.at[3]),
    ]
    for copy in small:
        copy.start()
    load = pltpu.make_async_copy(pop, f, in_sem.at[0])
    load.start()

    barrier = pltpu.get_barrier_semaphore()
    greeted = [(0, k) for k in range(1, leaves)]
    greeted += [(ds, dl) for ds in (1, -1) for dl in (0, 1, -1)]
    for ds, dl in greeted:
        pl.semaphore_signal(barrier, inc=1, device_id=device(ds, dl), device_id_type=MESH)

    for k in range(27):
        power = parts(k)
        scale = 0.5 ** sum(1 for p in power if p)
        third = (1.0 / 3.0) ** sum(1 for p in power if p == 2)
        rate = rates[k]
        coef[0, k] = jnp.full((8, 128), (1.0 - rate) * scale, F32)
        coef[1, k] = jnp.full((8, 128), rate * (scale * third), F32)

    for copy in small:
        copy.wait()
    for t in range(2):
        own_dest = m_dest[t]
        own_cells = m_cells[t : t + 1, :].astype(F32)
        own_force = m_forces[:, t, :]
        for k in range(leaves):
            chosen = own_dest == device(0, k)[1]
            masked = jnp.where(chosen, own_force, 0.0)
            target = m_recv if k == 0 else m_send
            target[t, k, 0:3, :] = masked
            target[t, k, 3:4, :] = own_cells
    pl.semaphore_wait(barrier, len(greeted))

    def marker_copy(t, k):
        return pltpu.make_async_remote_copy(
            src_ref=m_send.at[t, k], dst_ref=m_recv.at[t, k],
            send_sem=ms_sem.at[t, k], recv_sem=mr_sem.at[t, k],
            device_id=device(0, k), device_id_type=MESH,
        )

    for t in range(2):
        for k in range(1, leaves):
            marker_copy(t, k).start()

    def keep(k):
        return coef[0, k]

    def pull(k):
        return coef[1, k]

    load.wait()

    def relax_plane(x, carry):
        n = relax(forward([f[q, x] for q in range(27)]), keep, pull)
        for k in range(27):
            f[k, x] = n[k]
        return carry

    lax.fori_loop(0, wx, relax_plane, 0, unroll=2)

    def tile(v):
        return jnp.broadcast_to(v.astype(F32), (16, count)).astype(BF16)

    one = jnp.ones((16, count), BF16)
    zero = jnp.zeros((16, count), BF16)
    counted = [
        (lax.broadcasted_iota(jnp.int32, (16, count), 0) + 16 * g).astype(F32).astype(BF16)
        for g in range(16)
    ]

    def deposit(t):
        def spread(s):
            cell = m_recv[t, s, 3:4, :].astype(jnp.int32)
            row = tile((cell >> 7) & 63)
            column = tile(((cell >> 13) << 7) + (cell & 127))
            lanes = pl.ds(pl.multiple_of(s * count, 128), count)
            for g in range(16):
                hot_b[16 * g : 16 * g + 16, lanes] = jnp.where(counted[g] == column, one, zero)
            halves = []
            for d in range(3):
                amount = m_recv[t, s, d : d + 1, :]
                high = amount.astype(BF16).astype(F32)
                halves.append((64 * d, tile(high)))
                halves.append((64 * d + 192, tile(amount - high)))
            for g in range(4):
                is_row = counted[g] == row
                for start, half in halves:
                    hot_a[start + 16 * g : start + 16 * g + 16, lanes] = jnp.where(is_row, half, zero)

        spread(0)

        def arrived(s, carry):
            marker_copy(t, s).wait_recv()
            spread(s)
            return carry

        lax.fori_loop(1, leaves, arrived, 0)
        both = lax.dot_general(
            hot_a[...], hot_b[...], (((1,), (1,)), ((), ())), preferred_element_type=F32
        )
        total = both[0:192] + both[192:384]
        for d in range(3):
            for side in range(2):
                block = total[64 * d : 64 * d + 64, 128 * side : 128 * side + 128]
                force[d, 8 * side : 8 * side + 8] = block.reshape(8, 8, 128)

    def put(t, post, x, n):
        n = add_force(n, [force[d, x] for d in range(3)])
        values = backward(n)
        for q in range(27):
            _, cy, cz = parts(q)
            v = values[q]
            if cy != 1:
                v = pltpu.roll(v, 1 if cy == 2 else 127, axis=1)
            if cz != 1:
                v = pltpu.roll(v, 1 if cz == 2 else 7, axis=0)
            post[q, x + 1] = v
            if cz == 2:
                send_p[t, q // 3, x] = v[0:1]
            if cz == 0:
                send_m[t, q // 3, x] = v[7:8]

    def halo(t, post):
        low, high = zlo.at[t], zhi.at[t]
        up, down = send_p.at[t], send_m.at[t]
        last = wx - 1
        plan = [
            (post.at[18:27, wx], post.at[18:27, 0], (1, 0)),
            (post.at[0:9, 1], post.at[0:9, wx + 1], (-1, 0)),
            (up, low.at[:, 1 : wx + 1], (0, 1)),
            (down, high.at[:, 1 : wx + 1], (0, -1)),
            (up.at[6:9, last], low.at[6:9, 0], (1, 1)),
            (up.at[0:3, 0], low.at[0:3, wx + 1], (-1, 1)),
            (down.at[6:9, last], high.at[6:9, 0], (1, -1)),
            (down.at[0:3, 0], high.at[0:3, wx + 1], (-1, -1)),
        ]
        return [
            pltpu.make_async_remote_copy(
                src_ref=source, dst_ref=target,
                send_sem=hs_sem.at[t, i], recv_sem=hr_sem.at[t, i],
                device_id=device(*where), device_id_type=MESH,
            )
            for i, (source, target, where) in enumerate(plan)
        ]

    sublane = lax.broadcasted_iota(jnp.int32, (8, 128), 0)

    deposit(0)

    def put_plane(x, carry):
        put(0, pa, x, [f[k, x] for k in range(27)])
        return carry

    lax.fori_loop(0, wx, put_plane, 0, unroll=2)
    first = halo(0, pa)
    for copy in first:
        copy.start()
    deposit(1)
    for copy in first:
        copy.wait_recv()

    def whole_plane(x, carry):
        values = []
        for q in range(27):
            cx, _, cz = parts(q)
            at = x + (2 - cx)
            v = pa[q, at]
            if cz == 2:
                v = jnp.where(sublane == 0, zlo[0, q // 3, at], v)
            if cz == 0:
                v = jnp.where(sublane == 7, zhi[0, q // 3, at], v)
            values.append(v)
        put(1, pb, x, relax(forward(values), keep, pull))
        return carry

    lax.fori_loop(0, wx, whole_plane, 0, unroll=2)
    second = halo(1, pb)
    for copy in second:
        copy.start()
    for copy in second:
        copy.wait_recv()
    for copy in second:
        copy.wait_send()

    def close_plane(x, carry):
        for q in range(27):
            cx, _, cz = parts(q)
            at = x + (2 - cx)
            v = pb[q, at]
            if cz == 2:
                v = jnp.where(sublane == 0, zlo[1, q // 3, at], v)
            if cz == 0:
                v = jnp.where(sublane == 7, zhi[1, q // 3, at], v)
            out[q, x] = v
        return carry

    lax.fori_loop(0, wx, close_plane, 0, unroll=2)
    for copy in first:
        copy.wait_send()
    for t in range(2):
        for k in range(1, leaves):
            marker_copy(t, k).wait_send()


def body(spans, leaves, populations, relax_rates, marker_forces, marker_dest, marker_cells):
    steps, _, count = marker_forces.shape
    wx = populations.shape[1]
    anywhere = pl.BlockSpec(memory_space=pl.ANY)
    vmem = pltpu.VMEM
    dma = pltpu.SemaphoreType.DMA
    return pl.pallas_call(
        functools.partial(kernel, spans, leaves),
        out_shape=vmem(populations.shape, F32),
        in_specs=[anywhere, pl.BlockSpec(memory_space=pltpu.SMEM), anywhere, anywhere, anywhere],
        out_specs=pl.BlockSpec(memory_space=vmem),
        scratch_shapes=[
            vmem(populations.shape, F32),
            vmem((27, wx + 2, 8, 128), F32),
            vmem((27, wx + 2, 8, 128), F32),
            vmem((2, 27, 8, 128), F32),
            vmem((3, wx, 8, 128), F32),
            vmem((384, leaves * count), BF16),
            vmem((256, leaves * count), BF16),
            vmem((3, steps, count), F32),
            vmem((steps, 1, count), jnp.int32),
            vmem((steps, count), jnp.int32),
            vmem((steps, leaves, 4, count), F32),
            vmem((steps, leaves, 4, count), F32),
            vmem((steps, 9, wx, 1, 128), F32),
            vmem((steps, 9, wx, 1, 128), F32),
            vmem((steps, 9, wx + 2, 1, 128), F32),
            vmem((steps, 9, wx + 2, 1, 128), F32),
            dma((4,)),
            dma((steps, leaves)),
            dma((steps, leaves)),
            dma((steps, 8)),
            dma((steps, 8)),
        ],
        compiler_params=pltpu.CompilerParams(
            collective_id=0, has_side_effects=True, vmem_limit_bytes=60 * 1024 * 1024
        ),
        cost_estimate=pl.CostEstimate(
            flops=700 * 2 * populations.size // 27, bytes_accessed=8 * populations.size,
            transcendentals=0,
        ),
    )(
        populations, relax_rates, marker_forces.transpose(1, 0, 2),
        marker_dest.transpose(0, 2, 1), marker_cells,
    )


def solution(mesh):
    spans, leaves = mesh.shape["span"], mesh.shape["leaf"]
    placed = (
        P(None, "span", "leaf", None),
        P(),
        P(None, None, ("span", "leaf")),
        P(None, ("span", "leaf"), None),
        P(None, ("span", "leaf")),
    )
    return jax.shard_map(
        functools.partial(body, spans, leaves),
        mesh=mesh, in_specs=placed, out_specs=P(None, "span", "leaf", None), check_vma=False,
    )
```

```python
import functools

import jax
import jax.numpy as jnp
from jax import lax
from jax.experimental import pallas as pl
from jax.experimental.pallas import tpu as pltpu
from jax.sharding import PartitionSpec as P

MESH = pl.DeviceIdType.MESH
F32 = jnp.float32
BF16 = jnp.bfloat16
PIECES = 4


def parts(index):
    return index // 9, (index // 3) % 3, index % 3


def forward(values):
    for stride in (1, 3, 9):
        moved = list(values)
        for low in range(27):
            if (low // stride) % 3 == 0:
                a, b, c = (values[low + stride * i] for i in range(3))
                both = a + c
                moved[low] = both + b
                moved[low + stride] = c - a
                moved[low + 2 * stride] = both
        values = moved
    return values


def backward(values):
    for stride in (9, 3, 1):
        moved = list(values)
        for low in range(27):
            if (low // stride) % 3 == 0:
                a, b, c = (values[low + stride * i] for i in range(3))
                moved[low] = c - b
                moved[low + stride] = a - (c + c)
                moved[low + 2 * stride] = c + b
        values = moved
    return values


def relax(m, keep, pull):
    momentum = (m[9], m[3], m[1])
    squares = [v * v * (1.0 / 9.0) for v in momentum]
    result = []
    for k in range(27):
        power = parts(k)
        ones = [i for i in range(3) if power[i] == 1]
        if len(ones) == 3:
            result.append(keep(k) * m[k])
            continue
        if len(ones) == 2:
            target = momentum[ones[0]] * momentum[ones[1]] * (1.0 / 27.0)
        elif len(ones) == 1:
            target = momentum[ones[0]]
        else:
            target = m[0]
            for i in range(3):
                if power[i] == 2:
                    target = target + squares[i]
        result.append(keep(k) * m[k] + pull(k) * target)
    return result


def add_force(n, force):
    n = list(n)
    for k in range(27):
        power = parts(k)
        ones = [i for i in range(3) if power[i] == 1]
        if len(ones) == 1:
            twos = sum(1 for p in power if p == 2)
            factor = 0.5 * (0.5 / 3.0) ** twos
            n[k] = n[k] + factor * force[ones[0]]
    return n


def kernel(
    spans, leaves,
    pop, rates, forces, dest, cells, out,
    f, pa, faces, coef, force, hot_a, hot_b,
    m_forces, m_dest, m_cells, m_send, m_recv,
    send_p, send_m, zlo, zhi,
    in_sem, ms_sem, mr_sem, hs_sem, hr_sem,
):
    wx = pop.shape[1]
    count = cells.shape[1]
    me_s = lax.axis_index("span")
    me_l = lax.axis_index("leaf")

    def device(ds, dl):
        return (lax.rem(me_s + ds + spans, spans), lax.rem(me_l + dl + leaves, leaves))

    small = [
        pltpu.make_async_copy(forces, m_forces, in_sem.at[1]),
        pltpu.make_async_copy(dest, m_dest, in_sem.at[2]),
        pltpu.make_async_copy(cells, m_cells, in_sem.at[3]),
    ]
    for copy in small:
        copy.start()
    load = pltpu.make_async_copy(pop, f, in_sem.at[0])
    load.start()

    barrier = pltpu.get_barrier_semaphore()
    greeted = [(0, k) for k in range(1, leaves)]
    greeted += [(ds, dl) for ds in (1, -1) for dl in (0, 1, -1)]
    for ds, dl in greeted:
        pl.semaphore_signal(barrier, inc=1, device_id=device(ds, dl), device_id_type=MESH)

    for k in range(27):
        power = parts(k)
        scale = 0.5 ** sum(1 for p in power if p)
        third = (1.0 / 3.0) ** sum(1 for p in power if p == 2)
        rate = rates[k]
        coef[0, k] = jnp.full((8, 128), (1.0 - rate) * scale, F32)
        coef[1, k] = jnp.full((8, 128), rate * (scale * third), F32)

    for copy in small:
        copy.wait()
    for t in range(2):
        own_dest = m_dest[t]
        own_cells = m_cells[t : t + 1, :].astype(F32)
        own_force = m_forces[:, t, :]
        for k in range(leaves):
            chosen = own_dest == device(0, k)[1]
            masked = jnp.where(chosen, own_force, 0.0)
            target = m_recv if k == 0 else m_send
            target[t, k, 0:3, :] = masked
            target[t, k, 3:4, :] = own_cells
    pl.semaphore_wait(barrier, len(greeted))

    def marker_copy(t, k):
        return pltpu.make_async_remote_copy(
            src_ref=m_send.at[t, k], dst_ref=m_recv.at[t, k],
            send_sem=ms_sem.at[t, k], recv_sem=mr_sem.at[t, k],
            device_id=device(0, k), device_id_type=MESH,
        )

    for k in range(1, leaves):
        marker_copy(0, k).start()

    def keep(k):
        return coef[0, k]

    def pull(k):
        return coef[1, k]

    load.wait()

    def relax_plane(x, carry):
        n = relax(forward([f[q, x] for q in range(27)]), keep, pull)
        for k in range(27):
            f[k, x] = n[k]
        return carry

    lax.fori_loop(0, wx, relax_plane, 0, unroll=2)
    for k in range(1, leaves):
        marker_copy(1, k).start()

    def tile(v):
        return jnp.broadcast_to(v.astype(F32), (16, count)).astype(BF16)

    one = jnp.ones((16, count), BF16)
    zero = jnp.zeros((16, count), BF16)
    counted = [
        (lax.broadcasted_iota(jnp.int32, (16, count), 0) + 16 * g).astype(F32).astype(BF16)
        for g in range(16)
    ]

    def deposit(t):
        def spread(s):
            cell = m_recv[t, s, 3:4, :].astype(jnp.int32)
            row = tile((cell >> 7) & 63)
            column = tile(((cell >> 13) << 7) + (cell & 127))
            lanes = pl.ds(pl.multiple_of(s * count, 128), count)
            for g in range(16):
                hot_b[16 * g : 16 * g + 16, lanes] = jnp.where(counted[g] == column, one, zero)
            halves = []
            for d in range(3):
                amount = m_recv[t, s, d : d + 1, :]
                high = amount.astype(BF16).astype(F32)
                halves.append((64 * d, tile(high)))
                halves.append((64 * d + 192, tile(amount - high)))
            for g in range(4):
                is_row = counted[g] == row
                for start, half in halves:
                    hot_a[start + 16 * g : start + 16 * g + 16, lanes] = jnp.where(is_row, half, zero)

        spread(0)

        def arrived(s, carry):
            marker_copy(t, s).wait_recv()
            spread(s)
            return carry

        lax.fori_loop(1, leaves, arrived, 0)
        both = lax.dot_general(
            hot_a[...], hot_b[...], (((1,), (1,)), ((), ())), preferred_element_type=F32
        )
        total = both[0:192] + both[192:384]
        for d in range(3):
            for side in range(2):
                block = total[64 * d : 64 * d + 64, 128 * side : 128 * side + 128]
                force[d, 8 * side : 8 * side + 8] = block.reshape(8, 8, 128)

    def put(t, x, n):
        n = add_force(n, [force[d, x] for d in range(3)])
        values = backward(n)
        for q in range(27):
            cx, cy, cz = parts(q)
            v = values[q]
            if cy != 1:
                v = pltpu.roll(v, 1 if cy == 2 else 127, axis=1)
            if cz != 1:
                v = pltpu.roll(v, 1 if cz == 2 else 7, axis=0)
            if t == 0:
                pa[q, x + 1] = v
            elif cx == 0 and isinstance(x, int) and x == 0:
                faces[0, q] = v
            elif cx == 2 and isinstance(x, int) and x == last:
                faces[1, q - 18] = v
            else:
                out[q, x + (cx - 1)] = v
            if cz == 2:
                send_p[t, q // 3, x] = v[0:1]
            if cz == 0:
                send_m[t, q // 3, x] = v[7:8]

    def halo(t):
        low, high = zlo.at[t], zhi.at[t]
        up, down = send_p.at[t], send_m.at[t]
        if t == 0:
            plan = [
                (pa.at[18:27, wx], pa.at[18:27, 0], (1, 0)),
                (pa.at[0:9, 1], pa.at[0:9, wx + 1], (-1, 0)),
            ]
        else:
            plan = [
                (faces.at[1], out.at[18:27, 0], (1, 0)),
                (faces.at[0], out.at[0:9, last], (-1, 0)),
            ]
        plan += [
            (up.at[6:9, last], low.at[6:9, 0], (1, 1)),
            (up.at[0:3, 0], low.at[0:3, wx + 1], (-1, 1)),
            (down.at[6:9, last], high.at[6:9, 0], (1, -1)),
            (down.at[0:3, 0], high.at[0:3, wx + 1], (-1, -1)),
        ]
        for c in range(PIECES):
            at = slice(c * piece, (c + 1) * piece)
            to = slice(c * piece + 1, (c + 1) * piece + 1)
            plan.append((up.at[:, at], low.at[:, to], (0, 1)))
            plan.append((down.at[:, at], high.at[:, to], (0, -1)))
        return [
            pltpu.make_async_remote_copy(
                src_ref=source, dst_ref=target,
                send_sem=hs_sem.at[t, i], recv_sem=hr_sem.at[t, i],
                device_id=device(*where), device_id_type=MESH,
            )
            for i, (source, target, where) in enumerate(plan)
        ]

    def planes(plane, copies):
        plane(0, 0)
        plane(last, 0)
        for copy in copies[:6]:
            copy.start()
        for c in range(PIECES):
            start, stop = max(c * piece, 1), min((c + 1) * piece, last)
            lax.fori_loop(start, stop, plane, 0, unroll=2 if (stop - start) % 2 == 0 else True)
            for copy in copies[6 + 2 * c : 8 + 2 * c]:
                copy.start()

    last = wx - 1
    piece = wx // PIECES
    sublane = lax.broadcasted_iota(jnp.int32, (8, 128), 0)

    deposit(0)

    def put_plane(x, carry):
        put(0, x, [f[k, x] for k in range(27)])
        return carry

    first = halo(0)
    planes(put_plane, first)
    deposit(1)
    for copy in first:
        copy.wait_recv()

    def whole_plane(x, carry):
        values = []
        for q in range(27):
            cx, _, cz = parts(q)
            at = x + (2 - cx)
            v = pa[q, at]
            if cz == 2:
                v = jnp.where(sublane == 0, zlo[0, q // 3, at], v)
            if cz == 0:
                v = jnp.where(sublane == 7, zhi[0, q // 3, at], v)
            values.append(v)
        put(1, x, relax(forward(values), keep, pull))
        return carry

    second = halo(1)
    planes(whole_plane, second)
    for copy in second:
        copy.wait_recv()

    def close_plane(x, carry):
        for q in range(27):
            cx, _, cz = parts(q)
            at = x + (2 - cx)
            if cz == 2:
                out[q, x, 0:1] = zlo[1, q // 3, at]
            if cz == 0:
                out[q, x, 7:8] = zhi[1, q // 3, at]
        return carry

    lax.fori_loop(0, wx, close_plane, 0, unroll=2)
    for copy in second:
        copy.wait_send()
    for copy in first:
        copy.wait_send()
    for t in range(2):
        for k in range(1, leaves):
            marker_copy(t, k).wait_send()


def body(spans, leaves, populations, relax_rates, marker_forces, marker_dest, marker_cells):
    steps, _, count = marker_forces.shape
    wx = populations.shape[1]
    anywhere = pl.BlockSpec(memory_space=pl.ANY)
    vmem = pltpu.VMEM
    dma = pltpu.SemaphoreType.DMA
    return pl.pallas_call(
        functools.partial(kernel, spans, leaves),
        out_shape=vmem(populations.shape, F32),
        in_specs=[anywhere, pl.BlockSpec(memory_space=pltpu.SMEM), anywhere, anywhere, anywhere],
        out_specs=pl.BlockSpec(memory_space=vmem),
        scratch_shapes=[
            vmem(populations.shape, F32),
            vmem((27, wx + 2, 8, 128), F32),
            vmem((2, 9, 8, 128), F32),
            vmem((2, 27, 8, 128), F32),
            vmem((3, wx, 8, 128), F32),
            vmem((384, leaves * count), BF16),
            vmem((256, leaves * count), BF16),
            vmem((3, steps, count), F32),
            vmem((steps, 1, count), jnp.int32),
            vmem((steps, count), jnp.int32),
            vmem((steps, leaves, 4, count), F32),
            vmem((steps, leaves, 4, count), F32),
            vmem((steps, 9, wx, 1, 128), F32),
            vmem((steps, 9, wx, 1, 128), F32),
            vmem((steps, 9, wx + 2, 1, 128), F32),
            vmem((steps, 9, wx + 2, 1, 128), F32),
            dma((4,)),
            dma((steps, leaves)),
            dma((steps, leaves)),
            dma((steps, 6 + 2 * PIECES)),
            dma((steps, 6 + 2 * PIECES)),
        ],
        compiler_params=pltpu.CompilerParams(
            collective_id=0, has_side_effects=True, vmem_limit_bytes=60 * 1024 * 1024
        ),
        cost_estimate=pl.CostEstimate(
            flops=700 * 2 * populations.size // 27, bytes_accessed=8 * populations.size,
            transcendentals=0,
        ),
    )(
        populations, relax_rates, marker_forces.transpose(1, 0, 2),
        marker_dest.transpose(0, 2, 1), marker_cells,
    )


def solution(mesh):
    spans, leaves = mesh.shape["span"], mesh.shape["leaf"]
    placed = (
        P(None, "span", "leaf", None),
        P(),
        P(None, None, ("span", "leaf")),
        P(None, ("span", "leaf"), None),
        P(None, ("span", "leaf")),
    )
    return jax.shard_map(
        functools.partial(body, spans, leaves),
        mesh=mesh, in_specs=placed, out_specs=P(None, "span", "leaf", None), check_vma=False,
    )
```

```python
import functools

import jax
import jax.numpy as jnp
from jax import lax
from jax.experimental import pallas as pl
from jax.experimental.pallas import tpu as pltpu
from jax.sharding import PartitionSpec as P

MESH = pl.DeviceIdType.MESH
F32 = jnp.float32
BF16 = jnp.bfloat16
PIECES = 4


def parts(index):
    return index // 9, (index // 3) % 3, index % 3


def forward(values):
    for stride in (1, 3, 9):
        moved = list(values)
        for low in range(27):
            if (low // stride) % 3 == 0:
                a, b, c = (values[low + stride * i] for i in range(3))
                both = a + c
                moved[low] = both + b
                moved[low + stride] = c - a
                moved[low + 2 * stride] = both
        values = moved
    return values


def backward(values):
    for stride in (9, 3, 1):
        moved = list(values)
        for low in range(27):
            if (low // stride) % 3 == 0:
                a, b, c = (values[low + stride * i] for i in range(3))
                moved[low] = c - b
                moved[low + stride] = a - (c + c)
                moved[low + 2 * stride] = c + b
        values = moved
    return values


def relax(m, keep, pull):
    momentum = (m[9], m[3], m[1])
    squares = [v * v * (1.0 / 9.0) for v in momentum]
    result = []
    for k in range(27):
        power = parts(k)
        ones = [i for i in range(3) if power[i] == 1]
        if len(ones) == 3:
            result.append(keep(k) * m[k])
            continue
        if len(ones) == 2:
            target = momentum[ones[0]] * momentum[ones[1]] * (1.0 / 27.0)
        elif len(ones) == 1:
            target = momentum[ones[0]]
        else:
            target = m[0]
            for i in range(3):
                if power[i] == 2:
                    target = target + squares[i]
        result.append(keep(k) * m[k] + pull(k) * target)
    return result


def add_force(n, force):
    n = list(n)
    for k in range(27):
        power = parts(k)
        ones = [i for i in range(3) if power[i] == 1]
        if len(ones) == 1:
            twos = sum(1 for p in power if p == 2)
            factor = 0.5 * (0.5 / 3.0) ** twos
            n[k] = n[k] + factor * force[ones[0]]
    return n


def kernel(
    spans, leaves,
    pop, rates, forces, dest, cells, out,
    f, pa, faces, coef, force, hot_a, hot_b, both,
    m_forces, m_dest, m_cells, m_send, m_recv,
    send_p, send_m, zlo, zhi,
    in_sem, ms_sem, mr_sem, hs_sem, hr_sem,
):
    wx = pop.shape[1]
    count = cells.shape[1]
    me_s = lax.axis_index("span")
    me_l = lax.axis_index("leaf")

    def device(ds, dl):
        return (lax.rem(me_s + ds + spans, spans), lax.rem(me_l + dl + leaves, leaves))

    small = [
        pltpu.make_async_copy(forces, m_forces, in_sem.at[1]),
        pltpu.make_async_copy(dest, m_dest, in_sem.at[2]),
        pltpu.make_async_copy(cells, m_cells, in_sem.at[3]),
    ]
    for copy in small:
        copy.start()
    load = pltpu.make_async_copy(pop, f, in_sem.at[0])
    load.start()

    barrier = pltpu.get_barrier_semaphore()
    greeted = [(0, k) for k in range(1, leaves)]
    greeted += [(ds, dl) for ds in (1, -1) for dl in (0, 1, -1)]
    for ds, dl in greeted:
        pl.semaphore_signal(barrier, inc=1, device_id=device(ds, dl), device_id_type=MESH)

    for k in range(27):
        power = parts(k)
        scale = 0.5 ** sum(1 for p in power if p)
        third = (1.0 / 3.0) ** sum(1 for p in power if p == 2)
        rate = rates[k]
        coef[0, k] = jnp.full((8, 128), (1.0 - rate) * scale, F32)
        coef[1, k] = jnp.full((8, 128), rate * (scale * third), F32)

    for copy in small:
        copy.wait()
    for t in range(2):
        own_dest = m_dest[t]
        own_cells = m_cells[t : t + 1, :].astype(F32)
        own_force = m_forces[:, t, :]
        for k in range(leaves):
            chosen = own_dest == device(0, k)[1]
            masked = jnp.where(chosen, own_force, 0.0)
            target = m_recv if k == 0 else m_send
            target[t, k, 0:3, :] = masked
            target[t, k, 3:4, :] = own_cells
    pl.semaphore_wait(barrier, len(greeted))

    def marker_copy(t, k):
        return pltpu.make_async_remote_copy(
            src_ref=m_send.at[t, k], dst_ref=m_recv.at[t, k],
            send_sem=ms_sem.at[t, k], recv_sem=mr_sem.at[t, k],
            device_id=device(0, k), device_id_type=MESH,
        )

    for k in range(1, leaves):
        marker_copy(0, k).start()

    def keep(k):
        return coef[0, k]

    def pull(k):
        return coef[1, k]

    load.wait()

    def relax_plane(x, carry):
        n = relax(forward([f[q, x] for q in range(27)]), keep, pull)
        for k in range(27):
            f[k, x] = n[k]
        return carry

    lax.fori_loop(0, wx, relax_plane, 0, unroll=2)
    for k in range(1, leaves):
        marker_copy(1, k).start()

    def tile(v):
        return jnp.broadcast_to(v.astype(F32), (16, count)).astype(BF16)

    one = jnp.ones((16, count), BF16)
    zero = jnp.zeros((16, count), BF16)
    counted = [
        (lax.broadcasted_iota(jnp.int32, (16, count), 0) + 16 * g).astype(F32).astype(BF16)
        for g in range(16)
    ]

    def deposit(t):
        def spread(s, side):
            cell = m_recv[t, s, 3:4, :].astype(jnp.int32)
            row = tile((cell >> 7) & 63)
            column = tile(((cell >> 13) << 7) + (cell & 127))
            lanes = slice(side * count, (side + 1) * count)
            for g in range(16):
                hot_b[16 * g : 16 * g + 16, lanes] = jnp.where(counted[g] == column, one, zero)
            halves = []
            for d in range(3):
                amount = m_recv[t, s, d : d + 1, :]
                high = amount.astype(BF16).astype(F32)
                halves.append((64 * d, tile(high)))
                halves.append((64 * d + 192, tile(amount - high)))
            for g in range(4):
                is_row = counted[g] == row
                for start, half in halves:
                    hot_a[start + 16 * g : start + 16 * g + 16, lanes] = jnp.where(is_row, half, zero)

        def pair(p, carry):
            @pl.when(p > 0)
            def _():
                marker_copy(t, 2 * p).wait_recv()

            spread(2 * p, 0)
            marker_copy(t, 2 * p + 1).wait_recv()
            spread(2 * p + 1, 1)
            both[...] += lax.dot_general(
                hot_a[...], hot_b[...], (((1,), (1,)), ((), ())), preferred_element_type=F32
            )
            return carry

        both[...] = jnp.zeros_like(both)
        lax.fori_loop(0, leaves // 2, pair, 0)
        total = both[0:192] + both[192:384]
        for d in range(3):
            for side in range(2):
                block = total[64 * d : 64 * d + 64, 128 * side : 128 * side + 128]
                force[d, 8 * side : 8 * side + 8] = block.reshape(8, 8, 128)

    def put(t, x, n):
        n = add_force(n, [force[d, x] for d in range(3)])
        values = backward(n)
        for q in range(27):
            cx, cy, cz = parts(q)
            v = values[q]
            if cy != 1:
                v = pltpu.roll(v, 1 if cy == 2 else 127, axis=1)
            if cz != 1:
                v = pltpu.roll(v, 1 if cz == 2 else 7, axis=0)
            if t == 0:
                pa[q, x + 1] = v
            elif cx == 0 and isinstance(x, int) and x == 0:
                faces[0, q] = v
            elif cx == 2 and isinstance(x, int) and x == last:
                faces[1, q - 18] = v
            else:
                out[q, x + (cx - 1)] = v
            if cz == 2:
                send_p[t, q // 3, x] = v[0:1]
            if cz == 0:
                send_m[t, q // 3, x] = v[7:8]

    def halo(t):
        low, high = zlo.at[t], zhi.at[t]
        up, down = send_p.at[t], send_m.at[t]
        if t == 0:
            plan = [
                (pa.at[18:27, wx], pa.at[18:27, 0], (1, 0)),
                (pa.at[0:9, 1], pa.at[0:9, wx + 1], (-1, 0)),
            ]
        else:
            plan = [
                (faces.at[1], out.at[18:27, 0], (1, 0)),
                (faces.at[0], out.at[0:9, last], (-1, 0)),
            ]
        plan += [
            (up.at[6:9, last], low.at[6:9, 0], (1, 1)),
            (up.at[0:3, 0], low.at[0:3, wx + 1], (-1, 1)),
            (down.at[6:9, last], high.at[6:9, 0], (1, -1)),
            (down.at[0:3, 0], high.at[0:3, wx + 1], (-1, -1)),
        ]
        for c in range(PIECES):
            start = ends[c - 1] if c else 0
            at, to = slice(start, ends[c]), slice(start + 1, ends[c] + 1)
            plan.append((up.at[:, at], low.at[:, to], (0, 1)))
            plan.append((down.at[:, at], high.at[:, to], (0, -1)))
        return [
            pltpu.make_async_remote_copy(
                src_ref=source, dst_ref=target,
                send_sem=hs_sem.at[t, i], recv_sem=hr_sem.at[t, i],
                device_id=device(*where), device_id_type=MESH,
            )
            for i, (source, target, where) in enumerate(plan)
        ]

    def planes(plane, copies):
        if copies is first:
            lax.fori_loop(0, 2, lambda i, carry: plane(i * last, carry), 0)
        else:
            plane(0, 0)
            plane(last, 0)
        for copy in copies[:6]:
            copy.start()

        def pair(i, carry):
            plane(2 * i + 1, 0)
            plane(2 * i + 2, 0)
            for c in range(PIECES - 1):

                @pl.when(2 * i + 2 == ends[c] - 1)
                def _():
                    for copy in copies[6 + 2 * c : 8 + 2 * c]:
                        copy.start()

            return carry

        lax.fori_loop(0, wx // 2 - 1, pair, 0)
        for copy in copies[4 + 2 * PIECES :]:
            copy.start()

    last = wx - 1
    piece = wx // PIECES
    ends = [(c + 1) * piece + 1 for c in range(PIECES - 1)] + [wx]
    sublane = lax.broadcasted_iota(jnp.int32, (8, 128), 0)

    deposit(0)

    def put_plane(x, carry):
        put(0, x, [f[k, x] for k in range(27)])
        return carry

    first = halo(0)
    planes(put_plane, first)
    deposit(1)
    for copy in first:
        copy.wait_recv()

    def whole_plane(x, carry):
        values = []
        for q in range(27):
            cx, _, cz = parts(q)
            at = x + (2 - cx)
            v = pa[q, at]
            if cz == 2:
                v = jnp.where(sublane == 0, zlo[0, q // 3, at], v)
            if cz == 0:
                v = jnp.where(sublane == 7, zhi[0, q // 3, at], v)
            values.append(v)
        put(1, x, relax(forward(values), keep, pull))
        return carry

    second = halo(1)
    planes(whole_plane, second)
    for copy in second:
        copy.wait_recv()

    def close_plane(x, carry):
        for q in range(27):
            cx, _, cz = parts(q)
            at = x + (2 - cx)
            if cz == 2:
                out[q, x, 0:1] = zlo[1, q // 3, at]
            if cz == 0:
                out[q, x, 7:8] = zhi[1, q // 3, at]
        return carry

    lax.fori_loop(0, wx, close_plane, 0, unroll=2)
    for copy in second:
        copy.wait_send()
    for copy in first:
        copy.wait_send()
    for t in range(2):
        for k in range(1, leaves):
            marker_copy(t, k).wait_send()


def body(spans, leaves, populations, relax_rates, marker_forces, marker_dest, marker_cells):
    steps, _, count = marker_forces.shape
    wx = populations.shape[1]
    anywhere = pl.BlockSpec(memory_space=pl.ANY)
    vmem = pltpu.VMEM
    dma = pltpu.SemaphoreType.DMA
    return pl.pallas_call(
        functools.partial(kernel, spans, leaves),
        out_shape=vmem(populations.shape, F32),
        in_specs=[anywhere, pl.BlockSpec(memory_space=pltpu.SMEM), anywhere, anywhere, anywhere],
        out_specs=pl.BlockSpec(memory_space=vmem),
        scratch_shapes=[
            vmem(populations.shape, F32),
            vmem((27, wx + 2, 8, 128), F32),
            vmem((2, 9, 8, 128), F32),
            vmem((2, 27, 8, 128), F32),
            vmem((3, wx, 8, 128), F32),
            vmem((384, 2 * count), BF16),
            vmem((256, 2 * count), BF16),
            vmem((384, 256), F32),
            vmem((3, steps, count), F32),
            vmem((steps, 1, count), jnp.int32),
            vmem((steps, count), jnp.int32),
            vmem((steps, leaves, 4, count), F32),
            vmem((steps, leaves, 4, count), F32),
            vmem((steps, 9, wx, 1, 128), F32),
            vmem((steps, 9, wx, 1, 128), F32),
            vmem((steps, 9, wx + 2, 1, 128), F32),
            vmem((steps, 9, wx + 2, 1, 128), F32),
            dma((4,)),
            dma((steps, leaves)),
            dma((steps, leaves)),
            dma((steps, 6 + 2 * PIECES)),
            dma((steps, 6 + 2 * PIECES)),
        ],
        compiler_params=pltpu.CompilerParams(
            collective_id=0, has_side_effects=True, vmem_limit_bytes=60 * 1024 * 1024
        ),
        cost_estimate=pl.CostEstimate(
            flops=700 * 2 * populations.size // 27, bytes_accessed=8 * populations.size,
            transcendentals=0,
        ),
    )(
        populations, relax_rates, marker_forces.transpose(1, 0, 2),
        marker_dest.transpose(0, 2, 1), marker_cells,
    )


def solution(mesh):
    spans, leaves = mesh.shape["span"], mesh.shape["leaf"]
    placed = (
        P(None, "span", "leaf", None),
        P(),
        P(None, None, ("span", "leaf")),
        P(None, ("span", "leaf"), None),
        P(None, ("span", "leaf")),
    )
    return jax.shard_map(
        functools.partial(body, spans, leaves),
        mesh=mesh, in_specs=placed, out_specs=P(None, "span", "leaf", None), check_vma=False,
    )
```

```python
import functools

import jax
import jax.numpy as jnp
from jax import lax
from jax.experimental import pallas as pl
from jax.experimental.pallas import tpu as pltpu
from jax.sharding import PartitionSpec as P

MESH = pl.DeviceIdType.MESH
F32 = jnp.float32
BF16 = jnp.bfloat16
PIECES = 4


def parts(index):
    return index // 9, (index // 3) % 3, index % 3


def forward(values):
    for stride in (1, 3, 9):
        moved = list(values)
        for low in range(27):
            if (low // stride) % 3 == 0:
                a, b, c = (values[low + stride * i] for i in range(3))
                both = a + c
                moved[low] = both + b
                moved[low + stride] = c - a
                moved[low + 2 * stride] = both
        values = moved
    return values


def backward(values):
    for stride in (9, 3, 1):
        moved = list(values)
        for low in range(27):
            if (low // stride) % 3 == 0:
                a, b, c = (values[low + stride * i] for i in range(3))
                moved[low] = c - b
                moved[low + stride] = a - (c + c)
                moved[low + 2 * stride] = c + b
        values = moved
    return values


def relax(m, keep, pull):
    momentum = (m[9], m[3], m[1])
    squares = [v * v * (1.0 / 9.0) for v in momentum]
    result = []
    for k in range(27):
        power = parts(k)
        ones = [i for i in range(3) if power[i] == 1]
        if len(ones) == 3:
            result.append(keep(k) * m[k])
            continue
        if len(ones) == 2:
            target = momentum[ones[0]] * momentum[ones[1]] * (1.0 / 27.0)
        elif len(ones) == 1:
            target = momentum[ones[0]]
        else:
            target = m[0]
            for i in range(3):
                if power[i] == 2:
                    target = target + squares[i]
        result.append(keep(k) * m[k] + pull(k) * target)
    return result


def add_force(n, force):
    n = list(n)
    for k in range(27):
        power = parts(k)
        ones = [i for i in range(3) if power[i] == 1]
        if len(ones) == 1:
            twos = sum(1 for p in power if p == 2)
            factor = 0.5 * (0.5 / 3.0) ** twos
            n[k] = n[k] + factor * force[ones[0]]
    return n


def kernel(
    spans, leaves,
    pop, rates, forces, dest, cells, out,
    f, pa, faces, coef, force, hot_a, hot_b, both,
    m_forces, m_dest, m_cells, m_send, m_recv,
    send_p, send_m, zlo, zhi,
    in_sem, ms_sem, mr_sem, hs_sem, hr_sem,
):
    wx = pop.shape[1]
    count = cells.shape[1]
    me_s = lax.axis_index("span")
    me_l = lax.axis_index("leaf")

    def device(ds, dl):
        return (lax.rem(me_s + ds + spans, spans), lax.rem(me_l + dl + leaves, leaves))

    small = [
        pltpu.make_async_copy(forces, m_forces, in_sem.at[1]),
        pltpu.make_async_copy(dest, m_dest, in_sem.at[2]),
        pltpu.make_async_copy(cells, m_cells, in_sem.at[3]),
    ]
    for copy in small:
        copy.start()
    load = pltpu.make_async_copy(pop, f, in_sem.at[0])
    load.start()

    barrier = pltpu.get_barrier_semaphore()
    greeted = [(0, k) for k in range(1, leaves)]
    greeted += [(1, 0), (-1, 0)]
    for ds, dl in greeted:
        pl.semaphore_signal(barrier, inc=1, device_id=device(ds, dl), device_id_type=MESH)

    for k in range(27):
        power = parts(k)
        scale = 0.5 ** sum(1 for p in power if p)
        third = (1.0 / 3.0) ** sum(1 for p in power if p == 2)
        rate = rates[k]
        coef[0, k] = jnp.full((8, 128), (1.0 - rate) * scale, F32)
        coef[1, k] = jnp.full((8, 128), rate * (scale * third), F32)

    for copy in small:
        copy.wait()
    for t in range(2):
        own_dest = m_dest[t]
        own_cells = m_cells[t : t + 1, :].astype(F32)
        own_force = m_forces[:, t, :]
        for k in range(leaves):
            chosen = own_dest == device(0, k)[1]
            masked = jnp.where(chosen, own_force, 0.0)
            target = m_recv if k == 0 else m_send
            target[t, k, 0:3, :] = masked
            target[t, k, 3:4, :] = own_cells
    pl.semaphore_wait(barrier, len(greeted))

    def marker_copy(t, k):
        return pltpu.make_async_remote_copy(
            src_ref=m_send.at[t, k], dst_ref=m_recv.at[t, k],
            send_sem=ms_sem.at[t, k], recv_sem=mr_sem.at[t, k],
            device_id=device(0, k), device_id_type=MESH,
        )

    for k in range(1, leaves):
        marker_copy(0, k).start()

    def keep(k):
        return coef[0, k]

    def pull(k):
        return coef[1, k]

    load.wait()

    def relax_plane(x, carry):
        n = relax(forward([f[q, x] for q in range(27)]), keep, pull)
        for k in range(27):
            f[k, x] = n[k]
        return carry

    lax.fori_loop(0, wx, relax_plane, 0, unroll=2)
    for k in range(1, leaves):
        marker_copy(1, k).start()

    def tile(v):
        return jnp.broadcast_to(v.astype(F32), (16, count)).astype(BF16)

    one = jnp.ones((16, count), BF16)
    zero = jnp.zeros((16, count), BF16)
    counted = [
        (lax.broadcasted_iota(jnp.int32, (16, count), 0) + 16 * g).astype(F32).astype(BF16)
        for g in range(16)
    ]

    def deposit(t):
        def spread(s, side):
            cell = m_recv[t, s, 3:4, :].astype(jnp.int32)
            row = tile((cell >> 7) & 63)
            column = tile(((cell >> 13) << 7) + (cell & 127))
            lanes = slice(side * count, (side + 1) * count)
            for g in range(16):
                hot_b[16 * g : 16 * g + 16, lanes] = jnp.where(counted[g] == column, one, zero)
            halves = []
            for d in range(3):
                amount = m_recv[t, s, d : d + 1, :]
                high = amount.astype(BF16).astype(F32)
                halves.append((64 * d, tile(high)))
                halves.append((64 * d + 192, tile(amount - high)))
            for g in range(4):
                is_row = counted[g] == row
                for start, half in halves:
                    hot_a[start + 16 * g : start + 16 * g + 16, lanes] = jnp.where(is_row, half, zero)

        def pair(p, carry):
            @pl.when(p > 0)
            def _():
                marker_copy(t, 2 * p).wait_recv()

            spread(2 * p, 0)
            marker_copy(t, 2 * p + 1).wait_recv()
            spread(2 * p + 1, 1)
            both[...] += lax.dot_general(
                hot_a[...], hot_b[...], (((1,), (1,)), ((), ())), preferred_element_type=F32
            )
            return carry

        both[...] = jnp.zeros_like(both)
        lax.fori_loop(0, leaves // 2, pair, 0)
        total = both[0:192] + both[192:384]
        for d in range(3):
            for side in range(2):
                block = total[64 * d : 64 * d + 64, 128 * side : 128 * side + 128]
                force[d, 8 * side : 8 * side + 8] = block.reshape(8, 8, 128)

    def put(t, x, n):
        n = add_force(n, [force[d, x] for d in range(3)])
        values = backward(n)
        for q in range(27):
            cx, cy, cz = parts(q)
            v = values[q]
            if cy != 1:
                v = pltpu.roll(v, 1 if cy == 2 else 127, axis=1)
            if cz != 1:
                v = pltpu.roll(v, 1 if cz == 2 else 7, axis=0)
            if t == 0:
                pa[q, x + 1] = v
            elif cx == 0 and isinstance(x, int) and x == 0:
                faces[0, q] = v
            elif cx == 2 and isinstance(x, int) and x == last:
                faces[1, q - 18] = v
            else:
                out[q, x + (cx - 1)] = v
            if cz == 2:
                send_p[t, q // 3, x] = v[0:1]
            if cz == 0:
                send_m[t, q // 3, x] = v[7:8]

    def halo(t):
        low, high = zlo.at[t], zhi.at[t]
        up, down = send_p.at[t], send_m.at[t]
        if t == 0:
            plan = [
                (pa.at[18:27, wx], pa.at[18:27, 0], (1, 0)),
                (pa.at[0:9, 1], pa.at[0:9, wx + 1], (-1, 0)),
            ]
        else:
            plan = [
                (faces.at[1], out.at[18:27, 0], (1, 0)),
                (faces.at[0], out.at[0:9, last], (-1, 0)),
            ]
        plan += [
            (up.at[6:9, last], low.at[6:9, 0], (1, 1)),
            (up.at[0:3, 0], low.at[0:3, wx + 1], (-1, 1)),
            (down.at[6:9, last], high.at[6:9, 0], (1, -1)),
            (down.at[0:3, 0], high.at[0:3, wx + 1], (-1, -1)),
        ]
        for c in range(PIECES):
            start = ends[c - 1] if c else 0
            at, to = slice(start, ends[c]), slice(start + 1, ends[c] + 1)
            plan.append((up.at[:, at], low.at[:, to], (0, 1)))
            plan.append((down.at[:, at], high.at[:, to], (0, -1)))
        return [
            pltpu.make_async_remote_copy(
                src_ref=source, dst_ref=target,
                send_sem=hs_sem.at[t, i], recv_sem=hr_sem.at[t, i],
                device_id=device(*where), device_id_type=MESH,
            )
            for i, (source, target, where) in enumerate(plan)
        ]

    def planes(plane, copies):
        if copies is first:
            lax.fori_loop(0, 2, lambda i, carry: plane(i * last, carry), 0)
        else:
            plane(0, 0)
            plane(last, 0)
        for copy in copies[:6]:
            copy.start()

        def pair(i, carry):
            plane(2 * i + 1, 0)
            plane(2 * i + 2, 0)
            for c in range(PIECES - 1):

                @pl.when(2 * i + 2 == ends[c] - 1)
                def _():
                    for copy in copies[6 + 2 * c : 8 + 2 * c]:
                        copy.start()

            return carry

        lax.fori_loop(0, wx // 2 - 1, pair, 0)
        for copy in copies[4 + 2 * PIECES :]:
            copy.start()

    last = wx - 1
    piece = wx // PIECES
    ends = [(c + 1) * piece + 1 for c in range(PIECES - 1)] + [wx]
    sublane = lax.broadcasted_iota(jnp.int32, (8, 128), 0)

    deposit(0)

    def put_plane(x, carry):
        put(0, x, [f[k, x] for k in range(27)])
        return carry

    first = halo(0)
    planes(put_plane, first)
    deposit(1)
    for copy in first:
        copy.wait_recv()

    def whole_plane(x, carry):
        values = []
        for q in range(27):
            cx, _, cz = parts(q)
            at = x + (2 - cx)
            v = pa[q, at]
            if cz == 2:
                v = jnp.where(sublane == 0, zlo[0, q // 3, at], v)
            if cz == 0:
                v = jnp.where(sublane == 7, zhi[0, q // 3, at], v)
            values.append(v)
        put(1, x, relax(forward(values), keep, pull))
        return carry

    second = halo(1)
    planes(whole_plane, second)
    for copy in second:
        copy.wait_recv()

    def close_plane(x, carry):
        for q in range(27):
            cx, _, cz = parts(q)
            at = x + (2 - cx)
            if cz == 2:
                out[q, x, 0:1] = zlo[1, q // 3, at]
            if cz == 0:
                out[q, x, 7:8] = zhi[1, q // 3, at]
        return carry

    lax.fori_loop(0, wx, close_plane, 0, unroll=2)
    for copy in second:
        copy.wait_send()
    for copy in first:
        copy.wait_send()
    for t in range(2):
        for k in range(1, leaves):
            marker_copy(t, k).wait_send()


def body(spans, leaves, populations, relax_rates, marker_forces, marker_dest, marker_cells):
    steps, _, count = marker_forces.shape
    wx = populations.shape[1]
    anywhere = pl.BlockSpec(memory_space=pl.ANY)
    vmem = pltpu.VMEM
    dma = pltpu.SemaphoreType.DMA
    return pl.pallas_call(
        functools.partial(kernel, spans, leaves),
        out_shape=vmem(populations.shape, F32),
        in_specs=[anywhere, pl.BlockSpec(memory_space=pltpu.SMEM), anywhere, anywhere, anywhere],
        out_specs=pl.BlockSpec(memory_space=vmem),
        scratch_shapes=[
            vmem(populations.shape, F32),
            vmem((27, wx + 2, 8, 128), F32),
            vmem((2, 9, 8, 128), F32),
            vmem((2, 27, 8, 128), F32),
            vmem((3, wx, 8, 128), F32),
            vmem((384, 2 * count), BF16),
            vmem((256, 2 * count), BF16),
            vmem((384, 256), F32),
            vmem((3, steps, count), F32),
            vmem((steps, 1, count), jnp.int32),
            vmem((steps, count), jnp.int32),
            vmem((steps, leaves, 4, count), F32),
            vmem((steps, leaves, 4, count), F32),
            vmem((steps, 9, wx, 1, 128), F32),
            vmem((steps, 9, wx, 1, 128), F32),
            vmem((steps, 9, wx + 2, 1, 128), F32),
            vmem((steps, 9, wx + 2, 1, 128), F32),
            dma((4,)),
            dma((steps, leaves)),
            dma((steps, leaves)),
            dma((steps, 6 + 2 * PIECES)),
            dma((steps, 6 + 2 * PIECES)),
        ],
        compiler_params=pltpu.CompilerParams(
            collective_id=0, has_side_effects=True, vmem_limit_bytes=60 * 1024 * 1024
        ),
        cost_estimate=pl.CostEstimate(
            flops=700 * 2 * populations.size // 27, bytes_accessed=8 * populations.size,
            transcendentals=0,
        ),
    )(
        populations, relax_rates, marker_forces.transpose(1, 0, 2),
        marker_dest.transpose(0, 2, 1), marker_cells,
    )


def solution(mesh):
    spans, leaves = mesh.shape["span"], mesh.shape["leaf"]
    placed = (
        P(None, "span", "leaf", None),
        P(),
        P(None, None, ("span", "leaf")),
        P(None, ("span", "leaf"), None),
        P(None, ("span", "leaf")),
    )
    return jax.shard_map(
        functools.partial(body, spans, leaves),
        mesh=mesh, in_specs=placed, out_specs=P(None, "span", "leaf", None), check_vma=False,
    )
```

```python
import functools

import jax
import jax.numpy as jnp
from jax import lax
from jax.experimental import pallas as pl
from jax.experimental.pallas import tpu as pltpu
from jax.sharding import PartitionSpec as P

MESH = pl.DeviceIdType.MESH
F32 = jnp.float32
BF16 = jnp.bfloat16
PIECES = 4


def parts(index):
    return index // 9, (index // 3) % 3, index % 3


def forward(values):
    for stride in (1, 3, 9):
        moved = list(values)
        for low in range(27):
            if (low // stride) % 3 == 0:
                a, b, c = (values[low + stride * i] for i in range(3))
                both = a + c
                moved[low] = both + b
                moved[low + stride] = c - a
                moved[low + 2 * stride] = both
        values = moved
    return values


def backward(values):
    for stride in (9, 3, 1):
        moved = list(values)
        for low in range(27):
            if (low // stride) % 3 == 0:
                a, b, c = (values[low + stride * i] for i in range(3))
                moved[low] = c - b
                moved[low + stride] = a - (c + c)
                moved[low + 2 * stride] = c + b
        values = moved
    return values


def relax(m, keep, pull):
    momentum = (m[9], m[3], m[1])
    squares = [v * v * (1.0 / 9.0) for v in momentum]
    result = []
    for k in range(27):
        power = parts(k)
        ones = [i for i in range(3) if power[i] == 1]
        if len(ones) == 3:
            result.append(keep(k) * m[k])
            continue
        if len(ones) == 2:
            target = momentum[ones[0]] * momentum[ones[1]] * (1.0 / 27.0)
        elif len(ones) == 1:
            target = momentum[ones[0]]
        else:
            target = m[0]
            for i in range(3):
                if power[i] == 2:
                    target = target + squares[i]
        result.append(keep(k) * m[k] + pull(k) * target)
    return result


def add_force(n, force):
    n = list(n)
    for k in range(27):
        power = parts(k)
        ones = [i for i in range(3) if power[i] == 1]
        if len(ones) == 1:
            twos = sum(1 for p in power if p == 2)
            factor = 0.5 * (0.5 / 3.0) ** twos
            n[k] = n[k] + factor * force[ones[0]]
    return n


def kernel(
    spans, leaves,
    pop, rates, forces, dest, cells, out, zlo, zhi,
    f, pa, faces, coef, force, hot_a, hot_b, both,
    m_forces, m_dest, m_cells, m_send, m_recv,
    send_p, send_m,
    in_sem, ms_sem, mr_sem, hs_sem, hr_sem,
):
    wx = pop.shape[1]
    count = cells.shape[1]
    me_s = lax.axis_index("span")
    me_l = lax.axis_index("leaf")

    def device(ds, dl):
        return (lax.rem(me_s + ds + spans, spans), lax.rem(me_l + dl + leaves, leaves))

    small = [
        pltpu.make_async_copy(forces, m_forces, in_sem.at[1]),
        pltpu.make_async_copy(dest, m_dest, in_sem.at[2]),
        pltpu.make_async_copy(cells, m_cells, in_sem.at[3]),
    ]
    for copy in small:
        copy.start()
    load = pltpu.make_async_copy(pop, f, in_sem.at[0])
    load.start()

    barrier = pltpu.get_barrier_semaphore()
    greeted = [(0, k) for k in range(1, leaves)]
    greeted += [(1, 0), (-1, 0)]
    for ds, dl in greeted:
        pl.semaphore_signal(barrier, inc=1, device_id=device(ds, dl), device_id_type=MESH)

    for k in range(27):
        power = parts(k)
        scale = 0.5 ** sum(1 for p in power if p)
        third = (1.0 / 3.0) ** sum(1 for p in power if p == 2)
        rate = rates[k]
        coef[0, k] = jnp.full((8, 128), (1.0 - rate) * scale, F32)
        coef[1, k] = jnp.full((8, 128), rate * (scale * third), F32)

    for copy in small:
        copy.wait()
    for t in range(2):
        own_dest = m_dest[t]
        own_cells = m_cells[t : t + 1, :].astype(F32)
        own_force = m_forces[:, t, :]
        for k in range(leaves):
            chosen = own_dest == device(0, k)[1]
            masked = jnp.where(chosen, own_force, 0.0)
            target = m_recv if k == 0 else m_send
            target[t, k, 0:3, :] = masked
            target[t, k, 3:4, :] = own_cells
    pl.semaphore_wait(barrier, len(greeted))

    def marker_copy(t, k):
        return pltpu.make_async_remote_copy(
            src_ref=m_send.at[t, k], dst_ref=m_recv.at[t, k],
            send_sem=ms_sem.at[t, k], recv_sem=mr_sem.at[t, k],
            device_id=device(0, k), device_id_type=MESH,
        )

    for k in range(1, leaves):
        marker_copy(0, k).start()

    def keep(k):
        return coef[0, k]

    def pull(k):
        return coef[1, k]

    load.wait()

    def relax_plane(x, carry):
        n = relax(forward([f[q, x] for q in range(27)]), keep, pull)
        for k in range(27):
            f[k, x] = n[k]
        return carry

    lax.fori_loop(0, wx, relax_plane, 0, unroll=2)
    for k in range(1, leaves):
        marker_copy(1, k).start()

    def tile(v):
        return jnp.broadcast_to(v.astype(F32), (16, count)).astype(BF16)

    one = jnp.ones((16, count), BF16)
    zero = jnp.zeros((16, count), BF16)
    counted = [
        (lax.broadcasted_iota(jnp.int32, (16, count), 0) + 16 * g).astype(F32).astype(BF16)
        for g in range(16)
    ]

    def deposit(t):
        def spread(s, side):
            cell = m_recv[t, s, 3:4, :].astype(jnp.int32)
            row = tile((cell >> 7) & 63)
            column = tile(((cell >> 13) << 7) + (cell & 127))
            lanes = slice(side * count, (side + 1) * count)
            for g in range(16):
                hot_b[16 * g : 16 * g + 16, lanes] = jnp.where(counted[g] == column, one, zero)
            halves = []
            for d in range(3):
                amount = m_recv[t, s, d : d + 1, :]
                high = amount.astype(BF16).astype(F32)
                halves.append((64 * d, tile(high)))
                halves.append((64 * d + 192, tile(amount - high)))
            for g in range(4):
                is_row = counted[g] == row
                for start, half in halves:
                    hot_a[start + 16 * g : start + 16 * g + 16, lanes] = jnp.where(is_row, half, zero)

        def pair(p, carry):
            @pl.when(p > 0)
            def _():
                marker_copy(t, 2 * p).wait_recv()

            spread(2 * p, 0)
            marker_copy(t, 2 * p + 1).wait_recv()
            spread(2 * p + 1, 1)
            both[...] += lax.dot_general(
                hot_a[...], hot_b[...], (((1,), (1,)), ((), ())), preferred_element_type=F32
            )
            return carry

        both[...] = jnp.zeros_like(both)
        lax.fori_loop(0, leaves // 2, pair, 0)
        total = both[0:192] + both[192:384]
        for d in range(3):
            for side in range(2):
                block = total[64 * d : 64 * d + 64, 128 * side : 128 * side + 128]
                force[d, 8 * side : 8 * side + 8] = block.reshape(8, 8, 128)

    def put(t, x, n):
        n = add_force(n, [force[d, x] for d in range(3)])
        values = backward(n)
        for q in range(27):
            cx, cy, cz = parts(q)
            v = values[q]
            if cy != 1:
                v = pltpu.roll(v, 1 if cy == 2 else 127, axis=1)
            if cz != 1:
                v = pltpu.roll(v, 1 if cz == 2 else 7, axis=0)
            if t == 0:
                pa[q, x + 1] = v
            elif cx == 0 and isinstance(x, int) and x == 0:
                faces[0, q] = v
            elif cx == 2 and isinstance(x, int) and x == last:
                faces[1, q - 18] = v
            else:
                out[q, x + (cx - 1)] = v
            if cz == 2:
                send_p[t, q // 3, x] = v[0:1]
            if cz == 0:
                send_m[t, q // 3, x] = v[7:8]

    def halo(t):
        low, high = zlo.at[t], zhi.at[t]
        up, down = send_p.at[t], send_m.at[t]
        if t == 0:
            plan = [
                (pa.at[18:27, wx], pa.at[18:27, 0], (1, 0)),
                (pa.at[0:9, 1], pa.at[0:9, wx + 1], (-1, 0)),
            ]
        else:
            plan = [
                (faces.at[1], out.at[18:27, 0], (1, 0)),
                (faces.at[0], out.at[0:9, last], (-1, 0)),
            ]
        plan += [
            (up.at[6:9, last], low.at[6:9, 0], (1, 1)),
            (up.at[0:3, 0], low.at[0:3, wx + 1], (-1, 1)),
            (down.at[6:9, last], high.at[6:9, 0], (1, -1)),
            (down.at[0:3, 0], high.at[0:3, wx + 1], (-1, -1)),
        ]
        for c in range(PIECES):
            start = ends[c - 1] if c else 0
            at, to = slice(start, ends[c]), slice(start + 1, ends[c] + 1)
            plan.append((up.at[:, at], low.at[:, to], (0, 1)))
            plan.append((down.at[:, at], high.at[:, to], (0, -1)))
        return [
            pltpu.make_async_remote_copy(
                src_ref=source, dst_ref=target,
                send_sem=hs_sem.at[t, i], recv_sem=hr_sem.at[t, i],
                device_id=device(*where), device_id_type=MESH,
            )
            for i, (source, target, where) in enumerate(plan)
        ]

    def planes(plane, copies):
        if copies is first:
            lax.fori_loop(0, 2, lambda i, carry: plane(i * last, carry), 0)
        else:
            plane(0, 0)
            plane(last, 0)
        for copy in copies[:6]:
            copy.start()

        def pair(i, carry):
            plane(2 * i + 1, 0)
            plane(2 * i + 2, 0)
            for c in range(PIECES - 1):

                @pl.when(2 * i + 2 == ends[c] - 1)
                def _():
                    for copy in copies[6 + 2 * c : 8 + 2 * c]:
                        copy.start()

            return carry

        lax.fori_loop(0, wx // 2 - 1, pair, 0)
        for copy in copies[4 + 2 * PIECES :]:
            copy.start()

    last = wx - 1
    piece = wx // PIECES
    ends = [(c + 1) * piece + 1 for c in range(PIECES - 1)] + [wx]
    sublane = lax.broadcasted_iota(jnp.int32, (8, 128), 0)

    deposit(0)

    def put_plane(x, carry):
        put(0, x, [f[k, x] for k in range(27)])
        return carry

    first = halo(0)
    planes(put_plane, first)
    deposit(1)
    for copy in first:
        copy.wait_recv()

    def whole_plane(x, carry):
        values = []
        for q in range(27):
            cx, _, cz = parts(q)
            at = x + (2 - cx)
            v = pa[q, at]
            if cz == 2:
                v = jnp.where(sublane == 0, zlo[0, q // 3, at], v)
            if cz == 0:
                v = jnp.where(sublane == 7, zhi[0, q // 3, at], v)
            values.append(v)
        put(1, x, relax(forward(values), keep, pull))
        return carry

    second = halo(1)
    planes(whole_plane, second)
    for copy in second:
        copy.wait_recv()

    for copy in second:
        copy.wait_send()
    for copy in first:
        copy.wait_send()
    for t in range(2):
        for k in range(1, leaves):
            marker_copy(t, k).wait_send()


def close_kernel(inner, low, high, out, whole, sem):
    wx = inner.shape[1]
    sublane = lax.broadcasted_iota(jnp.int32, (8, 128), 0)

    def store(g):
        return pltpu.make_async_copy(
            whole.at[pl.ds(3 * g, 3)], out.at[pl.ds(3 * g, 3)], sem.at[g]
        )

    def group(g, carry):
        shift = 2 - g // 3
        for x in range(wx):
            at = x + shift
            whole[3 * g, x] = jnp.where(sublane == 7, high[1, g, at], inner[3 * g, x])
            whole[3 * g + 1, x] = inner[3 * g + 1, x]
            whole[3 * g + 2, x] = jnp.where(sublane == 0, low[1, g, at], inner[3 * g + 2, x])
        store(g).start()
        return carry

    lax.fori_loop(0, 9, group, 0)
    for g in range(9):
        store(g).wait()


def body(spans, leaves, populations, relax_rates, marker_forces, marker_dest, marker_cells):
    steps, _, count = marker_forces.shape
    wx = populations.shape[1]
    anywhere = pl.BlockSpec(memory_space=pl.ANY)
    vmem = pltpu.VMEM
    dma = pltpu.SemaphoreType.DMA
    inner, low, high = pl.pallas_call(
        functools.partial(kernel, spans, leaves),
        out_shape=[vmem(populations.shape, F32)] + [vmem((steps, 9, wx + 2, 1, 128), F32)] * 2,
        in_specs=[anywhere, pl.BlockSpec(memory_space=pltpu.SMEM), anywhere, anywhere, anywhere],
        out_specs=[pl.BlockSpec(memory_space=vmem)] * 3,
        scratch_shapes=[
            vmem(populations.shape, F32),
            vmem((27, wx + 2, 8, 128), F32),
            vmem((2, 9, 8, 128), F32),
            vmem((2, 27, 8, 128), F32),
            vmem((3, wx, 8, 128), F32),
            vmem((384, 2 * count), BF16),
            vmem((256, 2 * count), BF16),
            vmem((384, 256), F32),
            vmem((3, steps, count), F32),
            vmem((steps, 1, count), jnp.int32),
            vmem((steps, count), jnp.int32),
            vmem((steps, leaves, 4, count), F32),
            vmem((steps, leaves, 4, count), F32),
            vmem((steps, 9, wx, 1, 128), F32),
            vmem((steps, 9, wx, 1, 128), F32),
            dma((4,)),
            dma((steps, leaves)),
            dma((steps, leaves)),
            dma((steps, 6 + 2 * PIECES)),
            dma((steps, 6 + 2 * PIECES)),
        ],
        compiler_params=pltpu.CompilerParams(
            collective_id=0, has_side_effects=True, vmem_limit_bytes=60 * 1024 * 1024
        ),
        cost_estimate=pl.CostEstimate(
            flops=700 * 2 * populations.size // 27, bytes_accessed=8 * populations.size,
            transcendentals=0,
        ),
    )(
        populations, relax_rates, marker_forces.transpose(1, 0, 2),
        marker_dest.transpose(0, 2, 1), marker_cells,
    )
    return pl.pallas_call(
        close_kernel,
        out_shape=jax.ShapeDtypeStruct(populations.shape, F32),
        in_specs=[pl.BlockSpec(memory_space=vmem)] * 3,
        out_specs=anywhere,
        scratch_shapes=[vmem(populations.shape, F32), dma((9,))],
        compiler_params=pltpu.CompilerParams(vmem_limit_bytes=16 * 1024 * 1024),
        cost_estimate=pl.CostEstimate(
            flops=populations.size, bytes_accessed=4 * populations.size, transcendentals=0
        ),
    )(inner, low, high)


def solution(mesh):
    spans, leaves = mesh.shape["span"], mesh.shape["leaf"]
    placed = (
        P(None, "span", "leaf", None),
        P(),
        P(None, None, ("span", "leaf")),
        P(None, ("span", "leaf"), None),
        P(None, ("span", "leaf")),
    )
    return jax.shard_map(
        functools.partial(body, spans, leaves),
        mesh=mesh, in_specs=placed, out_specs=P(None, "span", "leaf", None), check_vma=False,
    )
```

```python
import functools

import jax
import jax.numpy as jnp
from jax import lax
from jax.experimental import pallas as pl
from jax.experimental.pallas import tpu as pltpu
from jax.sharding import PartitionSpec as P

MESH = pl.DeviceIdType.MESH
F32 = jnp.float32
BF16 = jnp.bfloat16
PIECES = 4


def parts(index):
    return index // 9, (index // 3) % 3, index % 3


def forward(values):
    for stride in (1, 3, 9):
        moved = list(values)
        for low in range(27):
            if (low // stride) % 3 == 0:
                a, b, c = (values[low + stride * i] for i in range(3))
                both = a + c
                moved[low] = both + b
                moved[low + stride] = c - a
                moved[low + 2 * stride] = both
        values = moved
    return values


def backward(values):
    for stride in (9, 3, 1):
        moved = list(values)
        for low in range(27):
            if (low // stride) % 3 == 0:
                a, b, c = (values[low + stride * i] for i in range(3))
                moved[low] = c - b
                moved[low + stride] = a - (c + c)
                moved[low + 2 * stride] = c + b
        values = moved
    return values


def relax(m, keep, pull):
    momentum = (m[9], m[3], m[1])
    squares = [v * v * (1.0 / 9.0) for v in momentum]
    result = []
    for k in range(27):
        power = parts(k)
        ones = [i for i in range(3) if power[i] == 1]
        if len(ones) == 3:
            result.append(keep(k) * m[k])
            continue
        if len(ones) == 2:
            target = momentum[ones[0]] * momentum[ones[1]] * (1.0 / 27.0)
        elif len(ones) == 1:
            target = momentum[ones[0]]
        else:
            target = m[0]
            for i in range(3):
                if power[i] == 2:
                    target = target + squares[i]
        result.append(keep(k) * m[k] + pull(k) * target)
    return result


def add_force(n, force):
    n = list(n)
    for k in range(27):
        power = parts(k)
        ones = [i for i in range(3) if power[i] == 1]
        if len(ones) == 1:
            twos = sum(1 for p in power if p == 2)
            factor = 0.5 * (0.5 / 3.0) ** twos
            n[k] = n[k] + factor * force[ones[0]]
    return n


def kernel(
    spans, leaves,
    pop, rates, forces, dest, cells, out, zlo, zhi,
    f, pa, faces, coef, force, hot_a, hot_b, both,
    m_forces, m_dest, m_cells, m_send, m_recv,
    send_p, send_m,
    in_sem, ms_sem, mr_sem, hs_sem, hr_sem,
):
    wx = pop.shape[1]
    count = cells.shape[1]
    me_s = lax.axis_index("span")
    me_l = lax.axis_index("leaf")

    def device(ds, dl):
        return (lax.rem(me_s + ds + spans, spans), lax.rem(me_l + dl + leaves, leaves))

    small = [
        pltpu.make_async_copy(forces, m_forces, in_sem.at[1]),
        pltpu.make_async_copy(dest, m_dest, in_sem.at[2]),
        pltpu.make_async_copy(cells, m_cells, in_sem.at[3]),
    ]
    for copy in small:
        copy.start()
    load = pltpu.make_async_copy(pop, f, in_sem.at[0])
    load.start()

    barrier = pltpu.get_barrier_semaphore()
    greeted = [(0, k) for k in range(1, leaves)]
    greeted += [(1, 0), (-1, 0)]
    for ds, dl in greeted:
        pl.semaphore_signal(barrier, inc=1, device_id=device(ds, dl), device_id_type=MESH)

    for k in range(27):
        power = parts(k)
        scale = 0.5 ** sum(1 for p in power if p)
        third = (1.0 / 3.0) ** sum(1 for p in power if p == 2)
        rate = rates[k]
        coef[0, k] = jnp.full((8, 128), (1.0 - rate) * scale, F32)
        coef[1, k] = jnp.full((8, 128), rate * (scale * third), F32)

    for copy in small:
        copy.wait()
    for t in range(2):
        own_dest = m_dest[t]
        own_cells = m_cells[t : t + 1, :].astype(F32)
        own_force = m_forces[:, t, :]
        for k in range(leaves):
            chosen = own_dest == device(0, k)[1]
            masked = jnp.where(chosen, own_force, 0.0)
            target = m_recv if k == 0 else m_send
            target[t, k, 0:3, :] = masked
            target[t, k, 3:4, :] = own_cells
    pl.semaphore_wait(barrier, len(greeted))

    def marker_copy(t, k):
        return pltpu.make_async_remote_copy(
            src_ref=m_send.at[t, k], dst_ref=m_recv.at[t, k],
            send_sem=ms_sem.at[t, k], recv_sem=mr_sem.at[t, k],
            device_id=device(0, k), device_id_type=MESH,
        )

    for k in range(1, leaves):
        marker_copy(0, k).start()

    def keep(k):
        return coef[0, k]

    def pull(k):
        return coef[1, k]

    load.wait()

    def relax_plane(x, carry):
        n = relax(forward([f[q, x] for q in range(27)]), keep, pull)
        for k in range(27):
            f[k, x] = n[k]
        return carry

    lax.fori_loop(0, wx, relax_plane, 0, unroll=2)
    for k in range(1, leaves):
        marker_copy(1, k).start()

    def tile(v):
        return jnp.broadcast_to(v.astype(F32), (16, count)).astype(BF16)

    one = jnp.ones((16, count), BF16)
    zero = jnp.zeros((16, count), BF16)
    counted = [
        (lax.broadcasted_iota(jnp.int32, (16, count), 0) + 16 * g).astype(F32).astype(BF16)
        for g in range(16)
    ]

    def deposit(t):
        def spread(s):
            a, b, side = hot_a.at[s // 2 % 2], hot_b.at[s // 2 % 2], s % 2
            cell = m_recv[t, s, 3:4, :].astype(jnp.int32)
            row = tile((cell >> 7) & 63)
            column = tile(((cell >> 13) << 7) + (cell & 127))
            lanes = slice(side * count, (side + 1) * count)
            for g in range(16):
                b[16 * g : 16 * g + 16, lanes] = jnp.where(counted[g] == column, one, zero)
            halves = []
            for d in range(3):
                amount = m_recv[t, s, d : d + 1, :]
                high = amount.astype(BF16).astype(F32)
                halves.append((64 * d, tile(high)))
                halves.append((64 * d + 192, tile(amount - high)))
            for g in range(4):
                is_row = counted[g] == row
                for start, half in halves:
                    a[start + 16 * g : start + 16 * g + 16, lanes] = jnp.where(is_row, half, zero)

        marker_copy(t, 1).wait_recv()
        spread(0)
        spread(1)
        for p in range(leaves // 2):
            ahead = [2 * p + 2, 2 * p + 3] if 2 * p + 2 < leaves else []
            for sender in ahead:
                marker_copy(t, sender).wait_recv()
            product = lax.dot_general(
                hot_a[p % 2], hot_b[p % 2], (((1,), (1,)), ((), ())), preferred_element_type=F32
            )
            both[...] = product if p == 0 else both[...] + product
            for sender in ahead:
                spread(sender)
        total = both[0:192] + both[192:384]
        for d in range(3):
            for side in range(2):
                block = total[64 * d : 64 * d + 64, 128 * side : 128 * side + 128]
                force[d, 8 * side : 8 * side + 8] = block.reshape(8, 8, 128)

    def put(t, x, n):
        n = add_force(n, [force[d, x] for d in range(3)])
        values = backward(n)
        for q in range(27):
            cx, cy, cz = parts(q)
            v = values[q]
            if cy != 1:
                v = pltpu.roll(v, 1 if cy == 2 else 127, axis=1)
            if cz != 1:
                v = pltpu.roll(v, 1 if cz == 2 else 7, axis=0)
            if t == 0:
                pa[q, x + 1] = v
            elif cx == 0 and isinstance(x, int) and x == 0:
                faces[0, q] = v
            elif cx == 2 and isinstance(x, int) and x == last:
                faces[1, q - 18] = v
            else:
                out[q, x + (cx - 1)] = v
            if cz == 2:
                send_p[t, q // 3, x] = v[0:1]
            if cz == 0:
                send_m[t, q // 3, x] = v[7:8]

    def halo(t):
        low, high = zlo.at[t], zhi.at[t]
        up, down = send_p.at[t], send_m.at[t]
        if t == 0:
            plan = [
                (pa.at[18:27, wx], pa.at[18:27, 0], (1, 0)),
                (pa.at[0:9, 1], pa.at[0:9, wx + 1], (-1, 0)),
            ]
        else:
            plan = [
                (faces.at[1], out.at[18:27, 0], (1, 0)),
                (faces.at[0], out.at[0:9, last], (-1, 0)),
            ]
        plan += [
            (up.at[6:9, last], low.at[6:9, 0], (1, 1)),
            (up.at[0:3, 0], low.at[0:3, wx + 1], (-1, 1)),
            (down.at[6:9, last], high.at[6:9, 0], (1, -1)),
            (down.at[0:3, 0], high.at[0:3, wx + 1], (-1, -1)),
        ]
        for c in range(PIECES):
            start = ends[c - 1] if c else 0
            at, to = slice(start, ends[c]), slice(start + 1, ends[c] + 1)
            plan.append((up.at[:, at], low.at[:, to], (0, 1)))
            plan.append((down.at[:, at], high.at[:, to], (0, -1)))
        return [
            pltpu.make_async_remote_copy(
                src_ref=source, dst_ref=target,
                send_sem=hs_sem.at[t, i], recv_sem=hr_sem.at[t, i],
                device_id=device(*where), device_id_type=MESH,
            )
            for i, (source, target, where) in enumerate(plan)
        ]

    def planes(plane, copies):
        if copies is first:
            lax.fori_loop(0, 2, lambda i, carry: plane(i * last, carry), 0)
        else:
            plane(0, 0)
            plane(last, 0)
        for copy in copies[:6]:
            copy.start()

        def pair(i, carry):
            plane(2 * i + 1, 0)
            plane(2 * i + 2, 0)
            for c in range(PIECES - 1):

                @pl.when(2 * i + 2 == ends[c] - 1)
                def _():
                    for copy in copies[6 + 2 * c : 8 + 2 * c]:
                        copy.start()

            return carry

        lax.fori_loop(0, wx // 2 - 1, pair, 0)
        for copy in copies[4 + 2 * PIECES :]:
            copy.start()

    last = wx - 1
    piece = wx // PIECES
    ends = [(c + 1) * piece + 1 for c in range(PIECES - 1)] + [wx]
    sublane = lax.broadcasted_iota(jnp.int32, (8, 128), 0)

    deposit(0)

    def put_plane(x, carry):
        put(0, x, [f[k, x] for k in range(27)])
        return carry

    first = halo(0)
    planes(put_plane, first)
    deposit(1)
    for copy in first:
        copy.wait_recv()

    def whole_plane(x, carry):
        values = []
        for q in range(27):
            cx, _, cz = parts(q)
            at = x + (2 - cx)
            v = pa[q, at]
            if cz == 2:
                v = jnp.where(sublane == 0, zlo[0, q // 3, at], v)
            if cz == 0:
                v = jnp.where(sublane == 7, zhi[0, q // 3, at], v)
            values.append(v)
        put(1, x, relax(forward(values), keep, pull))
        return carry

    second = halo(1)
    planes(whole_plane, second)
    for copy in second:
        copy.wait_recv()

    for copy in second:
        copy.wait_send()
    for copy in first:
        copy.wait_send()
    for t in range(2):
        for k in range(1, leaves):
            marker_copy(t, k).wait_send()


def close_kernel(inner, low, high, out, whole, sem):
    wx = inner.shape[1]
    sublane = lax.broadcasted_iota(jnp.int32, (8, 128), 0)

    def store(g):
        return pltpu.make_async_copy(
            whole.at[pl.ds(3 * g, 3)], out.at[pl.ds(3 * g, 3)], sem.at[g]
        )

    def group(g, carry):
        shift = 2 - g // 3
        for x in range(wx):
            at = x + shift
            whole[3 * g, x] = jnp.where(sublane == 7, high[1, g, at], inner[3 * g, x])
            whole[3 * g + 1, x] = inner[3 * g + 1, x]
            whole[3 * g + 2, x] = jnp.where(sublane == 0, low[1, g, at], inner[3 * g + 2, x])
        store(g).start()
        return carry

    lax.fori_loop(0, 9, group, 0)
    for g in range(9):
        store(g).wait()


def body(spans, leaves, populations, relax_rates, marker_forces, marker_dest, marker_cells):
    steps, _, count = marker_forces.shape
    wx = populations.shape[1]
    anywhere = pl.BlockSpec(memory_space=pl.ANY)
    vmem = pltpu.VMEM
    dma = pltpu.SemaphoreType.DMA
    inner, low, high = pl.pallas_call(
        functools.partial(kernel, spans, leaves),
        out_shape=[vmem(populations.shape, F32)] + [vmem((steps, 9, wx + 2, 1, 128), F32)] * 2,
        in_specs=[anywhere, pl.BlockSpec(memory_space=pltpu.SMEM), anywhere, anywhere, anywhere],
        out_specs=[pl.BlockSpec(memory_space=vmem)] * 3,
        scratch_shapes=[
            vmem(populations.shape, F32),
            vmem((27, wx + 2, 8, 128), F32),
            vmem((2, 9, 8, 128), F32),
            vmem((2, 27, 8, 128), F32),
            vmem((3, wx, 8, 128), F32),
            vmem((2, 384, 2 * count), BF16),
            vmem((2, 256, 2 * count), BF16),
            vmem((384, 256), F32),
            vmem((3, steps, count), F32),
            vmem((steps, 1, count), jnp.int32),
            vmem((steps, count), jnp.int32),
            vmem((steps, leaves, 4, count), F32),
            vmem((steps, leaves, 4, count), F32),
            vmem((steps, 9, wx, 1, 128), F32),
            vmem((steps, 9, wx, 1, 128), F32),
            dma((4,)),
            dma((steps, leaves)),
            dma((steps, leaves)),
            dma((steps, 6 + 2 * PIECES)),
            dma((steps, 6 + 2 * PIECES)),
        ],
        compiler_params=pltpu.CompilerParams(
            collective_id=0, has_side_effects=True, vmem_limit_bytes=60 * 1024 * 1024
        ),
        cost_estimate=pl.CostEstimate(
            flops=700 * 2 * populations.size // 27, bytes_accessed=8 * populations.size,
            transcendentals=0,
        ),
    )(
        populations, relax_rates, marker_forces.transpose(1, 0, 2),
        marker_dest.transpose(0, 2, 1), marker_cells,
    )
    return pl.pallas_call(
        close_kernel,
        out_shape=jax.ShapeDtypeStruct(populations.shape, F32),
        in_specs=[pl.BlockSpec(memory_space=vmem)] * 3,
        out_specs=anywhere,
        scratch_shapes=[vmem(populations.shape, F32), dma((9,))],
        compiler_params=pltpu.CompilerParams(vmem_limit_bytes=16 * 1024 * 1024),
        cost_estimate=pl.CostEstimate(
            flops=populations.size, bytes_accessed=4 * populations.size, transcendentals=0
        ),
    )(inner, low, high)


def solution(mesh):
    spans, leaves = mesh.shape["span"], mesh.shape["leaf"]
    placed = (
        P(None, "span", "leaf", None),
        P(),
        P(None, None, ("span", "leaf")),
        P(None, ("span", "leaf"), None),
        P(None, ("span", "leaf")),
    )
    return jax.shard_map(
        functools.partial(body, spans, leaves),
        mesh=mesh, in_specs=placed, out_specs=P(None, "span", "leaf", None), check_vma=False,
    )
```

```python
import functools

import jax
import jax.numpy as jnp
from jax import lax
from jax.experimental import pallas as pl
from jax.experimental.pallas import tpu as pltpu
from jax.sharding import PartitionSpec as P

MESH = pl.DeviceIdType.MESH
F32 = jnp.float32
BF16 = jnp.bfloat16
PIECES = 7


def parts(index):
    return index // 9, (index // 3) % 3, index % 3


def forward(values):
    for stride in (1, 3, 9):
        moved = list(values)
        for low in range(27):
            if (low // stride) % 3 == 0:
                a, b, c = (values[low + stride * i] for i in range(3))
                both = a + c
                moved[low] = both + b
                moved[low + stride] = c - a
                moved[low + 2 * stride] = both
        values = moved
    return values


def backward(values):
    for stride in (9, 3, 1):
        moved = list(values)
        for low in range(27):
            if (low // stride) % 3 == 0:
                a, b, c = (values[low + stride * i] for i in range(3))
                moved[low] = c - b
                moved[low + stride] = a - (c + c)
                moved[low + 2 * stride] = c + b
        values = moved
    return values


def relax(m, keep, pull):
    momentum = (m[9], m[3], m[1])
    squares = [v * v * (1.0 / 9.0) for v in momentum]
    result = []
    for k in range(27):
        power = parts(k)
        ones = [i for i in range(3) if power[i] == 1]
        if len(ones) == 3:
            result.append(keep(k) * m[k])
            continue
        if len(ones) == 2:
            target = momentum[ones[0]] * momentum[ones[1]] * (1.0 / 27.0)
        elif len(ones) == 1:
            target = momentum[ones[0]]
        else:
            target = m[0]
            for i in range(3):
                if power[i] == 2:
                    target = target + squares[i]
        result.append(keep(k) * m[k] + pull(k) * target)
    return result


def add_force(n, force):
    n = list(n)
    for k in range(27):
        power = parts(k)
        ones = [i for i in range(3) if power[i] == 1]
        if len(ones) == 1:
            twos = sum(1 for p in power if p == 2)
            factor = 0.5 * (0.5 / 3.0) ** twos
            n[k] = n[k] + factor * force[ones[0]]
    return n


def kernel(
    spans, leaves,
    pop, rates, forces, dest, cells, out, zlo, zhi,
    f, pa, faces, coef, force, hot_a, hot_b, both,
    m_forces, m_dest, m_cells, m_send, m_recv,
    send_p, send_m,
    in_sem, ms_sem, mr_sem, hs_sem, hr_sem,
):
    wx = pop.shape[1]
    count = cells.shape[1]
    me_s = lax.axis_index("span")
    me_l = lax.axis_index("leaf")

    def device(ds, dl):
        return (lax.rem(me_s + ds + spans, spans), lax.rem(me_l + dl + leaves, leaves))

    small = [
        pltpu.make_async_copy(forces, m_forces, in_sem.at[1]),
        pltpu.make_async_copy(dest, m_dest, in_sem.at[2]),
        pltpu.make_async_copy(cells, m_cells, in_sem.at[3]),
    ]
    for copy in small:
        copy.start()
    load = pltpu.make_async_copy(pop, f, in_sem.at[0])
    load.start()

    barrier = pltpu.get_barrier_semaphore()
    greeted = [(0, k) for k in range(1, leaves)]
    greeted += [(1, 0), (-1, 0)]
    for ds, dl in greeted:
        pl.semaphore_signal(barrier, inc=1, device_id=device(ds, dl), device_id_type=MESH)

    for k in range(27):
        power = parts(k)
        scale = 0.5 ** sum(1 for p in power if p)
        third = (1.0 / 3.0) ** sum(1 for p in power if p == 2)
        rate = rates[k]
        coef[0, k] = jnp.full((8, 128), (1.0 - rate) * scale, F32)
        coef[1, k] = jnp.full((8, 128), rate * (scale * third), F32)

    for copy in small:
        copy.wait()
    for t in range(2):
        own_dest = m_dest[t]
        own_cells = m_cells[t : t + 1, :].astype(F32)
        own_force = m_forces[:, t, :]
        for k in range(leaves):
            chosen = own_dest == device(0, k)[1]
            masked = jnp.where(chosen, own_force, 0.0)
            target = m_recv if k == 0 else m_send
            target[t, k, 0:3, :] = masked
            target[t, k, 3:4, :] = own_cells
    pl.semaphore_wait(barrier, len(greeted))

    def marker_copy(t, k):
        return pltpu.make_async_remote_copy(
            src_ref=m_send.at[t, k], dst_ref=m_recv.at[t, k],
            send_sem=ms_sem.at[t, k], recv_sem=mr_sem.at[t, k],
            device_id=device(0, k), device_id_type=MESH,
        )

    for k in range(1, leaves):
        marker_copy(0, k).start()

    def keep(k):
        return coef[0, k]

    def pull(k):
        return coef[1, k]

    load.wait()

    def relax_plane(x, carry):
        n = relax(forward([f[q, x] for q in range(27)]), keep, pull)
        for k in range(27):
            f[k, x] = n[k]
        return carry

    lax.fori_loop(0, wx, relax_plane, 0, unroll=2)
    for k in range(1, leaves):
        marker_copy(1, k).start()

    def tile(v):
        return jnp.broadcast_to(v.astype(F32), (16, count)).astype(BF16)

    one = jnp.ones((16, count), BF16)
    zero = jnp.zeros((16, count), BF16)
    counted = [
        (lax.broadcasted_iota(jnp.int32, (16, count), 0) + 16 * g).astype(F32).astype(BF16)
        for g in range(16)
    ]

    def deposit(t):
        def spread(s, side):
            cell = m_recv[t, s, 3:4, :].astype(jnp.int32)
            row = tile((cell >> 7) & 63)
            column = tile(((cell >> 13) << 7) + (cell & 127))
            lanes = slice(side * count, (side + 1) * count)
            for g in range(16):
                hot_b[16 * g : 16 * g + 16, lanes] = jnp.where(counted[g] == column, one, zero)
            halves = []
            for d in range(3):
                amount = m_recv[t, s, d : d + 1, :]
                high = amount.astype(BF16).astype(F32)
                halves.append((64 * d, tile(high)))
                halves.append((64 * d + 192, tile(amount - high)))
            for g in range(4):
                is_row = counted[g] == row
                for start, half in halves:
                    hot_a[start + 16 * g : start + 16 * g + 16, lanes] = jnp.where(is_row, half, zero)

        def pair(p, carry):
            @pl.when(p > 0)
            def _():
                marker_copy(t, 2 * p).wait_recv()

            spread(2 * p, 0)
            marker_copy(t, 2 * p + 1).wait_recv()
            spread(2 * p + 1, 1)
            both[...] += lax.dot_general(
                hot_a[...], hot_b[...], (((1,), (1,)), ((), ())), preferred_element_type=F32
            )
            return carry

        both[...] = jnp.zeros_like(both)
        lax.fori_loop(0, leaves // 2, pair, 0)
        total = both[0:192] + both[192:384]
        for d in range(3):
            for side in range(2):
                block = total[64 * d : 64 * d + 64, 128 * side : 128 * side + 128]
                force[d, 8 * side : 8 * side + 8] = block.reshape(8, 8, 128)

    def put(t, x, n):
        n = add_force(n, [force[d, x] for d in range(3)])
        values = backward(n)
        for q in range(27):
            cx, cy, cz = parts(q)
            v = values[q]
            if cy != 1:
                v = pltpu.roll(v, 1 if cy == 2 else 127, axis=1)
            if cz != 1:
                v = pltpu.roll(v, 1 if cz == 2 else 7, axis=0)
            if t == 0:
                pa[q, x + 1] = v
            elif cx == 0 and isinstance(x, int) and x == 0:
                faces[0, q] = v
            elif cx == 2 and isinstance(x, int) and x == last:
                faces[1, q - 18] = v
            else:
                out[q, x + (cx - 1)] = v
            if cz == 2:
                send_p[t, q // 3, x] = v[0:1]
            if cz == 0:
                send_m[t, q // 3, x] = v[7:8]

    def halo(t):
        low, high = zlo.at[t], zhi.at[t]
        up, down = send_p.at[t], send_m.at[t]
        if t == 0:
            plan = [
                (pa.at[18:27, wx], pa.at[18:27, 0], (1, 0)),
                (pa.at[0:9, 1], pa.at[0:9, wx + 1], (-1, 0)),
            ]
        else:
            plan = [
                (faces.at[1], out.at[18:27, 0], (1, 0)),
                (faces.at[0], out.at[0:9, last], (-1, 0)),
            ]
        plan += [
            (up.at[6:9, last], low.at[6:9, 0], (1, 1)),
            (up.at[0:3, 0], low.at[0:3, wx + 1], (-1, 1)),
            (down.at[6:9, last], high.at[6:9, 0], (1, -1)),
            (down.at[0:3, 0], high.at[0:3, wx + 1], (-1, -1)),
        ]
        for c in range(PIECES):
            start = ends[c - 1] if c else 0
            at, to = slice(start, ends[c]), slice(start + 1, ends[c] + 1)
            plan.append((up.at[:, at], low.at[:, to], (0, 1)))
            plan.append((down.at[:, at], high.at[:, to], (0, -1)))
        return [
            pltpu.make_async_remote_copy(
                src_ref=source, dst_ref=target,
                send_sem=hs_sem.at[t, i], recv_sem=hr_sem.at[t, i],
                device_id=device(*where), device_id_type=MESH,
            )
            for i, (source, target, where) in enumerate(plan)
        ]

    def planes(plane, copies):
        if copies is first:
            lax.fori_loop(0, 2, lambda i, carry: plane(i * last, carry), 0)
        else:
            plane(0, 0)
            plane(last, 0)
        for copy in copies[:6]:
            copy.start()

        def pair(i, carry):
            plane(2 * i + 1, 0)
            plane(2 * i + 2, 0)
            for c in range(PIECES - 1):

                @pl.when(2 * i + 2 == ends[c] - 1)
                def _():
                    for copy in copies[6 + 2 * c : 8 + 2 * c]:
                        copy.start()

            return carry

        lax.fori_loop(0, wx // 2 - 1, pair, 0)
        for copy in copies[4 + 2 * PIECES :]:
            copy.start()

    last = wx - 1
    piece = wx // PIECES
    ends = [(c + 1) * piece + 1 for c in range(PIECES - 1)] + [wx]
    sublane = lax.broadcasted_iota(jnp.int32, (8, 128), 0)

    deposit(0)

    def put_plane(x, carry):
        put(0, x, [f[k, x] for k in range(27)])
        return carry

    first = halo(0)
    planes(put_plane, first)
    deposit(1)
    for copy in first:
        copy.wait_recv()

    def whole_plane(x, carry):
        values = []
        for q in range(27):
            cx, _, cz = parts(q)
            at = x + (2 - cx)
            v = pa[q, at]
            if cz == 2:
                v = jnp.where(sublane == 0, zlo[0, q // 3, at], v)
            if cz == 0:
                v = jnp.where(sublane == 7, zhi[0, q // 3, at], v)
            values.append(v)
        put(1, x, relax(forward(values), keep, pull))
        return carry

    second = halo(1)
    planes(whole_plane, second)
    for copy in second:
        copy.wait_recv()

    for copy in second:
        copy.wait_send()
    for copy in first:
        copy.wait_send()
    for t in range(2):
        for k in range(1, leaves):
            marker_copy(t, k).wait_send()


def close_kernel(inner, low, high, out, whole, sem):
    wx = inner.shape[1]
    sublane = lax.broadcasted_iota(jnp.int32, (8, 128), 0)

    def store(g):
        return pltpu.make_async_copy(
            whole.at[pl.ds(3 * g, 3)], out.at[pl.ds(3 * g, 3)], sem.at[g]
        )

    def group(g, carry):
        shift = 2 - g // 3
        for x in range(wx):
            at = x + shift
            whole[3 * g, x] = jnp.where(sublane == 7, high[1, g, at], inner[3 * g, x])
            whole[3 * g + 1, x] = inner[3 * g + 1, x]
            whole[3 * g + 2, x] = jnp.where(sublane == 0, low[1, g, at], inner[3 * g + 2, x])
        store(g).start()
        return carry

    lax.fori_loop(0, 9, group, 0)
    for g in range(9):
        store(g).wait()


def body(spans, leaves, populations, relax_rates, marker_forces, marker_dest, marker_cells):
    steps, _, count = marker_forces.shape
    wx = populations.shape[1]
    anywhere = pl.BlockSpec(memory_space=pl.ANY)
    vmem = pltpu.VMEM
    dma = pltpu.SemaphoreType.DMA
    inner, low, high = pl.pallas_call(
        functools.partial(kernel, spans, leaves),
        out_shape=[vmem(populations.shape, F32)] + [vmem((steps, 9, wx + 2, 1, 128), F32)] * 2,
        in_specs=[anywhere, pl.BlockSpec(memory_space=pltpu.SMEM), anywhere, anywhere, anywhere],
        out_specs=[pl.BlockSpec(memory_space=vmem)] * 3,
        scratch_shapes=[
            vmem(populations.shape, F32),
            vmem((27, wx + 2, 8, 128), F32),
            vmem((2, 9, 8, 128), F32),
            vmem((2, 27, 8, 128), F32),
            vmem((3, wx, 8, 128), F32),
            vmem((384, 2 * count), BF16),
            vmem((256, 2 * count), BF16),
            vmem((384, 256), F32),
            vmem((3, steps, count), F32),
            vmem((steps, 1, count), jnp.int32),
            vmem((steps, count), jnp.int32),
            vmem((steps, leaves, 4, count), F32),
            vmem((steps, leaves, 4, count), F32),
            vmem((steps, 9, wx, 1, 128), F32),
            vmem((steps, 9, wx, 1, 128), F32),
            dma((4,)),
            dma((steps, leaves)),
            dma((steps, leaves)),
            dma((steps, 6 + 2 * PIECES)),
            dma((steps, 6 + 2 * PIECES)),
        ],
        compiler_params=pltpu.CompilerParams(
            collective_id=0, has_side_effects=True, vmem_limit_bytes=60 * 1024 * 1024
        ),
        cost_estimate=pl.CostEstimate(
            flops=700 * 2 * populations.size // 27, bytes_accessed=8 * populations.size,
            transcendentals=0,
        ),
    )(
        populations, relax_rates, marker_forces.transpose(1, 0, 2),
        marker_dest.transpose(0, 2, 1), marker_cells,
    )
    return pl.pallas_call(
        close_kernel,
        out_shape=jax.ShapeDtypeStruct(populations.shape, F32),
        in_specs=[pl.BlockSpec(memory_space=vmem)] * 3,
        out_specs=anywhere,
        scratch_shapes=[vmem(populations.shape, F32), dma((9,))],
        compiler_params=pltpu.CompilerParams(vmem_limit_bytes=16 * 1024 * 1024),
        cost_estimate=pl.CostEstimate(
            flops=populations.size, bytes_accessed=4 * populations.size, transcendentals=0
        ),
    )(inner, low, high)


def solution(mesh):
    spans, leaves = mesh.shape["span"], mesh.shape["leaf"]
    placed = (
        P(None, "span", "leaf", None),
        P(),
        P(None, None, ("span", "leaf")),
        P(None, ("span", "leaf"), None),
        P(None, ("span", "leaf")),
    )
    return jax.shard_map(
        functools.partial(body, spans, leaves),
        mesh=mesh, in_specs=placed, out_specs=P(None, "span", "leaf", None), check_vma=False,
    )
```

```python
import functools

import jax
import jax.numpy as jnp
from jax import lax
from jax.experimental import pallas as pl
from jax.experimental.pallas import tpu as pltpu
from jax.sharding import PartitionSpec as P

MESH = pl.DeviceIdType.MESH
F32 = jnp.float32
BF16 = jnp.bfloat16
PIECES = 4


def parts(index):
    return index // 9, (index // 3) % 3, index % 3


def forward(values):
    for stride in (1, 3, 9):
        moved = list(values)
        for low in range(27):
            if (low // stride) % 3 == 0:
                a, b, c = (values[low + stride * i] for i in range(3))
                both = a + c
                moved[low] = both + b
                moved[low + stride] = c - a
                moved[low + 2 * stride] = both
        values = moved
    return values


def backward(values):
    for stride in (9, 3, 1):
        moved = list(values)
        for low in range(27):
            if (low // stride) % 3 == 0:
                a, b, c = (values[low + stride * i] for i in range(3))
                moved[low] = c - b
                moved[low + stride] = a - (c + c)
                moved[low + 2 * stride] = c + b
        values = moved
    return values


def relax(m, keep, pull):
    momentum = (m[9], m[3], m[1])
    squares = [v * v * (1.0 / 9.0) for v in momentum]
    result = []
    for k in range(27):
        power = parts(k)
        ones = [i for i in range(3) if power[i] == 1]
        if len(ones) == 3:
            result.append(keep(k) * m[k])
            continue
        if len(ones) == 2:
            target = momentum[ones[0]] * momentum[ones[1]] * (1.0 / 27.0)
        elif len(ones) == 1:
            target = momentum[ones[0]]
        else:
            target = m[0]
            for i in range(3):
                if power[i] == 2:
                    target = target + squares[i]
        result.append(keep(k) * m[k] + pull(k) * target)
    return result


def add_force(n, force):
    n = list(n)
    for k in range(27):
        power = parts(k)
        ones = [i for i in range(3) if power[i] == 1]
        if len(ones) == 1:
            twos = sum(1 for p in power if p == 2)
            factor = 0.5 * (0.5 / 3.0) ** twos
            n[k] = n[k] + factor * force[ones[0]]
    return n


def kernel(
    spans, leaves,
    pop, rates, forces, dest, cells, out, zlo, zhi,
    f, pa, faces, coef, force, hot_a, hot_b, both,
    m_forces, m_dest, m_cells, m_send, m_recv,
    send_p, send_m,
    in_sem, ms_sem, mr_sem, hs_sem, hr_sem,
):
    wx = pop.shape[1]
    count = cells.shape[1]
    me_s = lax.axis_index("span")
    me_l = lax.axis_index("leaf")

    def device(ds, dl):
        return (lax.rem(me_s + ds + spans, spans), lax.rem(me_l + dl + leaves, leaves))

    small = [
        pltpu.make_async_copy(forces, m_forces, in_sem.at[1]),
        pltpu.make_async_copy(dest, m_dest, in_sem.at[2]),
        pltpu.make_async_copy(cells, m_cells, in_sem.at[3]),
    ]
    for copy in small:
        copy.start()
    load = pltpu.make_async_copy(pop, f, in_sem.at[0])
    load.start()

    barrier = pltpu.get_barrier_semaphore()
    greeted = [(0, k) for k in range(1, leaves)]
    greeted += [(1, 0), (-1, 0)]
    for ds, dl in greeted:
        pl.semaphore_signal(barrier, inc=1, device_id=device(ds, dl), device_id_type=MESH)

    for k in range(27):
        power = parts(k)
        scale = 0.5 ** sum(1 for p in power if p)
        third = (1.0 / 3.0) ** sum(1 for p in power if p == 2)
        rate = rates[k]
        coef[0, k] = jnp.full((8, 128), (1.0 - rate) * scale, F32)
        coef[1, k] = jnp.full((8, 128), rate * (scale * third), F32)

    for copy in small:
        copy.wait()
    for t in range(2):
        own_dest = m_dest[t]
        own_cells = m_cells[t : t + 1, :].astype(F32)
        own_force = m_forces[:, t, :]
        for k in range(leaves):
            chosen = own_dest == device(0, k)[1]
            masked = jnp.where(chosen, own_force, 0.0)
            target = m_recv if k == 0 else m_send
            target[t, k, 0:3, :] = masked
            target[t, k, 3:4, :] = own_cells
    pl.semaphore_wait(barrier, len(greeted))

    def marker_copy(t, k):
        return pltpu.make_async_remote_copy(
            src_ref=m_send.at[t, k], dst_ref=m_recv.at[t, k],
            send_sem=ms_sem.at[t, k], recv_sem=mr_sem.at[t, k],
            device_id=device(0, k), device_id_type=MESH,
        )

    for k in range(1, leaves):
        marker_copy(0, k).start()

    def keep(k):
        return coef[0, k]

    def pull(k):
        return coef[1, k]

    load.wait()

    def relax_plane(x, carry):
        n = relax(forward([f[q, x] for q in range(27)]), keep, pull)
        for k in range(27):
            f[k, x] = n[k]
        return carry

    lax.fori_loop(0, wx, relax_plane, 0, unroll=2)
    for k in range(1, leaves):
        marker_copy(1, k).start()

    def tile(v):
        return jnp.broadcast_to(v.astype(F32), (16, count)).astype(BF16)

    one = jnp.ones((16, count), BF16)
    zero = jnp.zeros((16, count), BF16)
    counted = [
        (lax.broadcasted_iota(jnp.int32, (16, count), 0) + 16 * g).astype(F32).astype(BF16)
        for g in range(16)
    ]

    def deposit(t):
        def spread(s, side):
            cell = m_recv[t, s, 3:4, :].astype(jnp.int32)
            row = tile((cell >> 7) & 63)
            column = tile(((cell >> 13) << 7) + (cell & 127))
            lanes = slice(side * count, (side + 1) * count)
            for g in range(16):
                hot_b[16 * g : 16 * g + 16, lanes] = jnp.where(counted[g] == column, one, zero)
            halves = []
            for d in range(3):
                amount = m_recv[t, s, d : d + 1, :]
                high = amount.astype(BF16).astype(F32)
                halves.append((64 * d, tile(high)))
                halves.append((64 * d + 192, tile(amount - high)))
            for g in range(4):
                is_row = counted[g] == row
                for start, half in halves:
                    hot_a[start + 16 * g : start + 16 * g + 16, lanes] = jnp.where(is_row, half, zero)

        def pair(p, carry):
            @pl.when(p > 0)
            def _():
                marker_copy(t, 2 * p).wait_recv()

            spread(2 * p, 0)
            marker_copy(t, 2 * p + 1).wait_recv()
            spread(2 * p + 1, 1)
            both[...] += lax.dot_general(
                hot_a[...], hot_b[...], (((1,), (1,)), ((), ())), preferred_element_type=F32
            )
            return carry

        both[...] = jnp.zeros_like(both)
        lax.fori_loop(0, leaves // 2, pair, 0)
        total = both[0:192] + both[192:384]
        for d in range(3):
            for side in range(2):
                block = total[64 * d : 64 * d + 64, 128 * side : 128 * side + 128]
                force[d, 8 * side : 8 * side + 8] = block.reshape(8, 8, 128)

    def put(t, x, n):
        n = add_force(n, [force[d, x] for d in range(3)])
        values = backward(n)
        for q in range(27):
            cx, cy, cz = parts(q)
            v = values[q]
            if cy != 1:
                v = pltpu.roll(v, 1 if cy == 2 else 127, axis=1)
            if cz != 1:
                v = pltpu.roll(v, 1 if cz == 2 else 7, axis=0)
            if t == 0:
                pa[q, x + 1] = v
            elif cx == 0 and isinstance(x, int) and x == 0:
                faces[0, q] = v
            elif cx == 2 and isinstance(x, int) and x == last:
                faces[1, q - 18] = v
            else:
                out[q, x + (cx - 1)] = v
            if cz == 2:
                send_p[t, q // 3, x] = v[0:1]
            if cz == 0:
                send_m[t, q // 3, x] = v[7:8]

    def halo(t):
        low, high = zlo.at[t], zhi.at[t]
        up, down = send_p.at[t], send_m.at[t]
        if t == 0:
            plan = [
                (pa.at[18:27, wx], pa.at[18:27, 0], (1, 0)),
                (pa.at[0:9, 1], pa.at[0:9, wx + 1], (-1, 0)),
            ]
        else:
            plan = [
                (faces.at[1], out.at[18:27, 0], (1, 0)),
                (faces.at[0], out.at[0:9, last], (-1, 0)),
            ]
        plan += [
            (up.at[6:9, last], low.at[6:9, 0], (1, 1)),
            (up.at[0:3, 0], low.at[0:3, wx + 1], (-1, 1)),
            (down.at[6:9, last], high.at[6:9, 0], (1, -1)),
            (down.at[0:3, 0], high.at[0:3, wx + 1], (-1, -1)),
        ]
        for c in range(PIECES):
            start = ends[c - 1] if c else 0
            at, to = slice(start, ends[c]), slice(start + 1, ends[c] + 1)
            plan.append((up.at[:, at], low.at[:, to], (0, 1)))
            plan.append((down.at[:, at], high.at[:, to], (0, -1)))
        return [
            pltpu.make_async_remote_copy(
                src_ref=source, dst_ref=target,
                send_sem=hs_sem.at[t, i], recv_sem=hr_sem.at[t, i],
                device_id=device(*where), device_id_type=MESH,
            )
            for i, (source, target, where) in enumerate(plan)
        ]

    def planes(plane, copies):
        if copies is first:
            lax.fori_loop(0, 2, lambda i, carry: plane(i * last, carry), 0)
        else:
            plane(0, 0)
            plane(last, 0)
        for copy in copies[:6]:
            copy.start()

        def pair(i, carry):
            plane(2 * i + 1, 0)
            plane(2 * i + 2, 0)
            for c in range(PIECES - 1):

                @pl.when(2 * i + 2 == ends[c] - 1)
                def _():
                    for copy in copies[6 + 2 * c : 8 + 2 * c]:
                        copy.start()

            return carry

        lax.fori_loop(0, wx // 2 - 1, pair, 0)
        for copy in copies[4 + 2 * PIECES :]:
            copy.start()

    last = wx - 1
    piece = wx // PIECES
    ends = [(c + 1) * piece + 1 for c in range(PIECES - 1)] + [wx]
    sublane = lax.broadcasted_iota(jnp.int32, (8, 128), 0)

    deposit(0)

    def put_plane(x, carry):
        put(0, x, [f[k, x] for k in range(27)])
        return carry

    first = halo(0)
    planes(put_plane, first)
    deposit(1)
    for copy in first:
        copy.wait_recv()

    def whole_plane(x, carry):
        values = []
        for q in range(27):
            cx, _, cz = parts(q)
            at = x + (2 - cx)
            v = pa[q, at]
            if cz == 2:
                v = jnp.where(sublane == 0, zlo[0, q // 3, at], v)
            if cz == 0:
                v = jnp.where(sublane == 7, zhi[0, q // 3, at], v)
            values.append(v)
        put(1, x, relax(forward(values), keep, pull))
        return carry

    second = halo(1)
    planes(whole_plane, second)
    for copy in first:
        copy.wait_send()
    for t in range(2):
        for k in range(1, leaves):
            marker_copy(t, k).wait_send()
    for copy in second:
        copy.wait_send()
    for copy in second:
        copy.wait_recv()


def close_kernel(inner, low, high, out, whole, sem):
    wx = inner.shape[1]
    sublane = lax.broadcasted_iota(jnp.int32, (8, 128), 0)

    def store(g):
        return pltpu.make_async_copy(
            whole.at[pl.ds(3 * g, 3)], out.at[pl.ds(3 * g, 3)], sem.at[g]
        )

    def group(g, carry):
        shift = 2 - g // 3
        for x in range(wx):
            at = x + shift
            whole[3 * g, x] = jnp.where(sublane == 7, high[1, g, at], inner[3 * g, x])
            whole[3 * g + 1, x] = inner[3 * g + 1, x]
            whole[3 * g + 2, x] = jnp.where(sublane == 0, low[1, g, at], inner[3 * g + 2, x])
        store(g).start()
        return carry

    lax.fori_loop(0, 9, group, 0)
    for g in range(9):
        store(g).wait()


def body(spans, leaves, populations, relax_rates, marker_forces, marker_dest, marker_cells):
    steps, _, count = marker_forces.shape
    wx = populations.shape[1]
    anywhere = pl.BlockSpec(memory_space=pl.ANY)
    vmem = pltpu.VMEM
    dma = pltpu.SemaphoreType.DMA
    inner, low, high = pl.pallas_call(
        functools.partial(kernel, spans, leaves),
        out_shape=[vmem(populations.shape, F32)] + [vmem((steps, 9, wx + 2, 1, 128), F32)] * 2,
        in_specs=[anywhere, pl.BlockSpec(memory_space=pltpu.SMEM), anywhere, anywhere, anywhere],
        out_specs=[pl.BlockSpec(memory_space=vmem)] * 3,
        scratch_shapes=[
            vmem(populations.shape, F32),
            vmem((27, wx + 2, 8, 128), F32),
            vmem((2, 9, 8, 128), F32),
            vmem((2, 27, 8, 128), F32),
            vmem((3, wx, 8, 128), F32),
            vmem((384, 2 * count), BF16),
            vmem((256, 2 * count), BF16),
            vmem((384, 256), F32),
            vmem((3, steps, count), F32),
            vmem((steps, 1, count), jnp.int32),
            vmem((steps, count), jnp.int32),
            vmem((steps, leaves, 4, count), F32),
            vmem((steps, leaves, 4, count), F32),
            vmem((steps, 9, wx, 1, 128), F32),
            vmem((steps, 9, wx, 1, 128), F32),
            dma((4,)),
            dma((steps, leaves)),
            dma((steps, leaves)),
            dma((steps, 6 + 2 * PIECES)),
            dma((steps, 6 + 2 * PIECES)),
        ],
        compiler_params=pltpu.CompilerParams(
            collective_id=0, has_side_effects=True, vmem_limit_bytes=60 * 1024 * 1024
        ),
        cost_estimate=pl.CostEstimate(
            flops=700 * 2 * populations.size // 27, bytes_accessed=8 * populations.size,
            transcendentals=0,
        ),
    )(
        populations, relax_rates, marker_forces.transpose(1, 0, 2),
        marker_dest.transpose(0, 2, 1), marker_cells,
    )
    return pl.pallas_call(
        close_kernel,
        out_shape=jax.ShapeDtypeStruct(populations.shape, F32),
        in_specs=[pl.BlockSpec(memory_space=vmem)] * 3,
        out_specs=anywhere,
        scratch_shapes=[vmem(populations.shape, F32), dma((9,))],
        compiler_params=pltpu.CompilerParams(vmem_limit_bytes=16 * 1024 * 1024),
        cost_estimate=pl.CostEstimate(
            flops=populations.size, bytes_accessed=4 * populations.size, transcendentals=0
        ),
    )(inner, low, high)


def solution(mesh):
    spans, leaves = mesh.shape["span"], mesh.shape["leaf"]
    placed = (
        P(None, "span", "leaf", None),
        P(),
        P(None, None, ("span", "leaf")),
        P(None, ("span", "leaf"), None),
        P(None, ("span", "leaf")),
    )
    return jax.shard_map(
        functools.partial(body, spans, leaves),
        mesh=mesh, in_specs=placed, out_specs=P(None, "span", "leaf", None), check_vma=False,
    )
```

```python
import functools

import jax
import jax.numpy as jnp
from jax import lax
from jax.experimental import pallas as pl
from jax.experimental.pallas import tpu as pltpu
from jax.sharding import PartitionSpec as P

MESH = pl.DeviceIdType.MESH
F32 = jnp.float32
BF16 = jnp.bfloat16
PIECES = 2


def parts(index):
    return index // 9, (index // 3) % 3, index % 3


def forward(values):
    for stride in (1, 3, 9):
        moved = list(values)
        for low in range(27):
            if (low // stride) % 3 == 0:
                a, b, c = (values[low + stride * i] for i in range(3))
                both = a + c
                moved[low] = both + b
                moved[low + stride] = c - a
                moved[low + 2 * stride] = both
        values = moved
    return values


def backward(values):
    for stride in (9, 3, 1):
        moved = list(values)
        for low in range(27):
            if (low // stride) % 3 == 0:
                a, b, c = (values[low + stride * i] for i in range(3))
                moved[low] = c - b
                moved[low + stride] = a - (c + c)
                moved[low + 2 * stride] = c + b
        values = moved
    return values


def relax(m, keep, pull):
    momentum = (m[9], m[3], m[1])
    squares = [v * v * (1.0 / 9.0) for v in momentum]
    result = []
    for k in range(27):
        power = parts(k)
        ones = [i for i in range(3) if power[i] == 1]
        if len(ones) == 3:
            result.append(keep(k) * m[k])
            continue
        if len(ones) == 2:
            target = momentum[ones[0]] * momentum[ones[1]] * (1.0 / 27.0)
        elif len(ones) == 1:
            target = momentum[ones[0]]
        else:
            target = m[0]
            for i in range(3):
                if power[i] == 2:
                    target = target + squares[i]
        result.append(keep(k) * m[k] + pull(k) * target)
    return result


def add_force(n, force):
    n = list(n)
    for k in range(27):
        power = parts(k)
        ones = [i for i in range(3) if power[i] == 1]
        if len(ones) == 1:
            twos = sum(1 for p in power if p == 2)
            factor = 0.5 * (0.5 / 3.0) ** twos
            n[k] = n[k] + factor * force[ones[0]]
    return n


def kernel(
    spans, leaves,
    pop, rates, forces, dest, cells, out, zlo, zhi,
    f, pa, faces, coef, force, hot_a, hot_b, both,
    m_forces, m_dest, m_cells, m_send, m_recv,
    send_p, send_m,
    in_sem, ms_sem, mr_sem, hs_sem, hr_sem,
):
    wx = pop.shape[1]
    count = cells.shape[1]
    me_s = lax.axis_index("span")
    me_l = lax.axis_index("leaf")

    def device(ds, dl):
        return (lax.rem(me_s + ds + spans, spans), lax.rem(me_l + dl + leaves, leaves))

    small = [
        pltpu.make_async_copy(forces, m_forces, in_sem.at[1]),
        pltpu.make_async_copy(dest, m_dest, in_sem.at[2]),
        pltpu.make_async_copy(cells, m_cells, in_sem.at[3]),
    ]
    for copy in small:
        copy.start()
    load = pltpu.make_async_copy(pop, f, in_sem.at[0])
    load.start()

    barrier = pltpu.get_barrier_semaphore()
    greeted = [(0, k) for k in range(1, leaves)]
    greeted += [(1, 0), (-1, 0)]
    for ds, dl in greeted:
        pl.semaphore_signal(barrier, inc=1, device_id=device(ds, dl), device_id_type=MESH)

    for k in range(27):
        power = parts(k)
        scale = 0.5 ** sum(1 for p in power if p)
        third = (1.0 / 3.0) ** sum(1 for p in power if p == 2)
        rate = rates[k]
        coef[0, k] = jnp.full((8, 128), (1.0 - rate) * scale, F32)
        coef[1, k] = jnp.full((8, 128), rate * (scale * third), F32)

    for copy in small:
        copy.wait()
    for t in range(2):
        own_dest = m_dest[t]
        own_cells = m_cells[t : t + 1, :].astype(F32)
        own_force = m_forces[:, t, :]
        for k in range(leaves):
            chosen = own_dest == device(0, k)[1]
            masked = jnp.where(chosen, own_force, 0.0)
            target = m_recv if k == 0 else m_send
            target[t, k, 0:3, :] = masked
            target[t, k, 3:4, :] = own_cells
    pl.semaphore_wait(barrier, len(greeted))

    def marker_copy(t, k):
        return pltpu.make_async_remote_copy(
            src_ref=m_send.at[t, k], dst_ref=m_recv.at[t, k],
            send_sem=ms_sem.at[t, k], recv_sem=mr_sem.at[t, k],
            device_id=device(0, k), device_id_type=MESH,
        )

    for k in range(1, leaves):
        marker_copy(0, k).start()

    def keep(k):
        return coef[0, k]

    def pull(k):
        return coef[1, k]

    load.wait()

    def relax_plane(x, carry):
        n = relax(forward([f[q, x] for q in range(27)]), keep, pull)
        for k in range(27):
            f[k, x] = n[k]
        return carry

    lax.fori_loop(0, wx, relax_plane, 0, unroll=2)
    for k in range(1, leaves):
        marker_copy(1, k).start()

    def tile(v):
        return jnp.broadcast_to(v.astype(F32), (16, count)).astype(BF16)

    one = jnp.ones((16, count), BF16)
    zero = jnp.zeros((16, count), BF16)
    counted = [
        (lax.broadcasted_iota(jnp.int32, (16, count), 0) + 16 * g).astype(F32).astype(BF16)
        for g in range(16)
    ]

    def deposit(t):
        def spread(s, side):
            cell = m_recv[t, s, 3:4, :].astype(jnp.int32)
            row = tile((cell >> 7) & 63)
            column = tile(((cell >> 13) << 7) + (cell & 127))
            lanes = slice(side * count, (side + 1) * count)
            for g in range(16):
                hot_b[16 * g : 16 * g + 16, lanes] = jnp.where(counted[g] == column, one, zero)
            halves = []
            for d in range(3):
                amount = m_recv[t, s, d : d + 1, :]
                high = amount.astype(BF16).astype(F32)
                halves.append((64 * d, tile(high)))
                halves.append((64 * d + 192, tile(amount - high)))
            for g in range(4):
                is_row = counted[g] == row
                for start, half in halves:
                    hot_a[start + 16 * g : start + 16 * g + 16, lanes] = jnp.where(is_row, half, zero)

        def pair(p, carry):
            @pl.when(p > 0)
            def _():
                marker_copy(t, 2 * p).wait_recv()

            spread(2 * p, 0)
            marker_copy(t, 2 * p + 1).wait_recv()
            spread(2 * p + 1, 1)
            both[...] += lax.dot_general(
                hot_a[...], hot_b[...], (((1,), (1,)), ((), ())), preferred_element_type=F32
            )
            return carry

        both[...] = jnp.zeros_like(both)
        lax.fori_loop(0, leaves // 2, pair, 0)
        total = both[0:192] + both[192:384]
        for d in range(3):
            for side in range(2):
                block = total[64 * d : 64 * d + 64, 128 * side : 128 * side + 128]
                force[d, 8 * side : 8 * side + 8] = block.reshape(8, 8, 128)

    def put(t, x, n):
        n = add_force(n, [force[d, x] for d in range(3)])
        values = backward(n)
        for q in range(27):
            cx, cy, cz = parts(q)
            v = values[q]
            if cy != 1:
                v = pltpu.roll(v, 1 if cy == 2 else 127, axis=1)
            if cz != 1:
                v = pltpu.roll(v, 1 if cz == 2 else 7, axis=0)
            if t == 0:
                pa[q, x + 1] = v
            elif cx == 0 and isinstance(x, int) and x == 0:
                faces[0, q] = v
            elif cx == 2 and isinstance(x, int) and x == last:
                faces[1, q - 18] = v
            else:
                out[q, x + (cx - 1)] = v
            if cz == 2:
                send_p[t, q // 3, x] = v[0:1]
            if cz == 0:
                send_m[t, q // 3, x] = v[7:8]

    def halo(t):
        low, high = zlo.at[t], zhi.at[t]
        up, down = send_p.at[t], send_m.at[t]
        if t == 0:
            plan = [
                (pa.at[18:27, wx], pa.at[18:27, 0], (1, 0)),
                (pa.at[0:9, 1], pa.at[0:9, wx + 1], (-1, 0)),
            ]
        else:
            plan = [
                (faces.at[1], out.at[18:27, 0], (1, 0)),
                (faces.at[0], out.at[0:9, last], (-1, 0)),
            ]
        plan += [
            (up.at[6:9, last], low.at[6:9, 0], (1, 1)),
            (up.at[0:3, 0], low.at[0:3, wx + 1], (-1, 1)),
            (down.at[6:9, last], high.at[6:9, 0], (1, -1)),
            (down.at[0:3, 0], high.at[0:3, wx + 1], (-1, -1)),
        ]
        for c in range(PIECES):
            start = ends[c - 1] if c else 0
            at, to = slice(start, ends[c]), slice(start + 1, ends[c] + 1)
            plan.append((up.at[:, at], low.at[:, to], (0, 1)))
            plan.append((down.at[:, at], high.at[:, to], (0, -1)))
        return [
            pltpu.make_async_remote_copy(
                src_ref=source, dst_ref=target,
                send_sem=hs_sem.at[t, i], recv_sem=hr_sem.at[t, i],
                device_id=device(*where), device_id_type=MESH,
            )
            for i, (source, target, where) in enumerate(plan)
        ]

    def planes(plane, copies):
        if copies is first:
            lax.fori_loop(0, 2, lambda i, carry: plane(i * last, carry), 0)
        else:
            plane(0, 0)
            plane(last, 0)
        for copy in copies[:6]:
            copy.start()

        def pair(i, carry):
            plane(2 * i + 1, 0)
            plane(2 * i + 2, 0)
            for c in range(PIECES - 1):

                @pl.when(2 * i + 2 == ends[c] - 1)
                def _():
                    for copy in copies[6 + 2 * c : 8 + 2 * c]:
                        copy.start()

            return carry

        lax.fori_loop(0, wx // 2 - 1, pair, 0)
        for copy in copies[4 + 2 * PIECES :]:
            copy.start()

    last = wx - 1
    piece = wx // PIECES
    ends = [(c + 1) * piece + 1 for c in range(PIECES - 1)] + [wx]
    sublane = lax.broadcasted_iota(jnp.int32, (8, 128), 0)

    deposit(0)

    def put_plane(x, carry):
        put(0, x, [f[k, x] for k in range(27)])
        return carry

    first = halo(0)
    planes(put_plane, first)
    deposit(1)
    for copy in first:
        copy.wait_recv()

    def whole_plane(x, carry):
        values = []
        for q in range(27):
            cx, _, cz = parts(q)
            at = x + (2 - cx)
            v = pa[q, at]
            if cz == 2:
                v = jnp.where(sublane == 0, zlo[0, q // 3, at], v)
            if cz == 0:
                v = jnp.where(sublane == 7, zhi[0, q // 3, at], v)
            values.append(v)
        put(1, x, relax(forward(values), keep, pull))
        return carry

    second = halo(1)
    planes(whole_plane, second)
    for copy in first:
        copy.wait_send()
    for t in range(2):
        for k in range(1, leaves):
            marker_copy(t, k).wait_send()
    for copy in second:
        copy.wait_send()
    for copy in second:
        copy.wait_recv()


def close_kernel(inner, low, high, out, whole, sem):
    wx = inner.shape[1]
    sublane = lax.broadcasted_iota(jnp.int32, (8, 128), 0)

    def store(g):
        return pltpu.make_async_copy(
            whole.at[pl.ds(3 * g, 3)], out.at[pl.ds(3 * g, 3)], sem.at[g]
        )

    def group(g, carry):
        shift = 2 - g // 3
        for x in range(wx):
            at = x + shift
            whole[3 * g, x] = jnp.where(sublane == 7, high[1, g, at], inner[3 * g, x])
            whole[3 * g + 1, x] = inner[3 * g + 1, x]
            whole[3 * g + 2, x] = jnp.where(sublane == 0, low[1, g, at], inner[3 * g + 2, x])
        store(g).start()
        return carry

    lax.fori_loop(0, 9, group, 0)
    for g in range(9):
        store(g).wait()


def body(spans, leaves, populations, relax_rates, marker_forces, marker_dest, marker_cells):
    steps, _, count = marker_forces.shape
    wx = populations.shape[1]
    anywhere = pl.BlockSpec(memory_space=pl.ANY)
    vmem = pltpu.VMEM
    dma = pltpu.SemaphoreType.DMA
    inner, low, high = pl.pallas_call(
        functools.partial(kernel, spans, leaves),
        out_shape=[vmem(populations.shape, F32)] + [vmem((steps, 9, wx + 2, 1, 128), F32)] * 2,
        in_specs=[anywhere, pl.BlockSpec(memory_space=pltpu.SMEM), anywhere, anywhere, anywhere],
        out_specs=[pl.BlockSpec(memory_space=vmem)] * 3,
        scratch_shapes=[
            vmem(populations.shape, F32),
            vmem((27, wx + 2, 8, 128), F32),
            vmem((2, 9, 8, 128), F32),
            vmem((2, 27, 8, 128), F32),
            vmem((3, wx, 8, 128), F32),
            vmem((384, 2 * count), BF16),
            vmem((256, 2 * count), BF16),
            vmem((384, 256), F32),
            vmem((3, steps, count), F32),
            vmem((steps, 1, count), jnp.int32),
            vmem((steps, count), jnp.int32),
            vmem((steps, leaves, 4, count), F32),
            vmem((steps, leaves, 4, count), F32),
            vmem((steps, 9, wx, 1, 128), F32),
            vmem((steps, 9, wx, 1, 128), F32),
            dma((4,)),
            dma((steps, leaves)),
            dma((steps, leaves)),
            dma((steps, 6 + 2 * PIECES)),
            dma((steps, 6 + 2 * PIECES)),
        ],
        compiler_params=pltpu.CompilerParams(
            collective_id=0, has_side_effects=True, vmem_limit_bytes=60 * 1024 * 1024
        ),
        cost_estimate=pl.CostEstimate(
            flops=700 * 2 * populations.size // 27, bytes_accessed=8 * populations.size,
            transcendentals=0,
        ),
    )(
        populations, relax_rates, marker_forces.transpose(1, 0, 2),
        marker_dest.transpose(0, 2, 1), marker_cells,
    )
    return pl.pallas_call(
        close_kernel,
        out_shape=jax.ShapeDtypeStruct(populations.shape, F32),
        in_specs=[pl.BlockSpec(memory_space=vmem)] * 3,
        out_specs=anywhere,
        scratch_shapes=[vmem(populations.shape, F32), dma((9,))],
        compiler_params=pltpu.CompilerParams(vmem_limit_bytes=16 * 1024 * 1024),
        cost_estimate=pl.CostEstimate(
            flops=populations.size, bytes_accessed=4 * populations.size, transcendentals=0
        ),
    )(inner, low, high)


def solution(mesh):
    spans, leaves = mesh.shape["span"], mesh.shape["leaf"]
    placed = (
        P(None, "span", "leaf", None),
        P(),
        P(None, None, ("span", "leaf")),
        P(None, ("span", "leaf"), None),
        P(None, ("span", "leaf")),
    )
    return jax.shard_map(
        functools.partial(body, spans, leaves),
        mesh=mesh, in_specs=placed, out_specs=P(None, "span", "leaf", None), check_vma=False,
    )
```
